256 devices in a mesh: items: 16 (over z_hi, x), events: 16 (over y, z_lo, core).
Axes of the slice: x: 4, y: 4, z: 8 (z_hi: 4, z_lo: 2; z = z_hi * 2 + z_lo), core: 2. Of those that a mesh axis runs over, the one named last changes fastest.
Arguments:
- history: bfloat16 [16, 2048, 1024], P('items', 'events'), may hold values from -6 to 6
- actions: int32 [16, 2048], P('items', 'events'), may hold values from 0 to 15
- action_table: bfloat16 [16, 1024], replicated, may hold values from -3 to 3
- lengths: int32 [16], P('items'), may hold values from 512 to 2048, as said below
- input_gain: float32 [1024], replicated, may hold values from 0.25 to 1.75
- input_weight: bfloat16 [1024, 4096], replicated, may hold values from -0.1875 to 0.1875
- output_gain: float32 [1024], replicated, may hold values from 0.25 to 1.75
- output_weight: bfloat16 [1024, 1024], replicated, may hold values from -0.1875 to 0.1875
- item_codes: int32 [32768, 256], P(('items', 'events')), may hold values from 0 to 65535
- item_scale: float32 [32768, 8], P(('items', 'events')), may hold values from 0.006 to 0.06
- gate_first: bfloat16 [64, 128], replicated, may hold values from -0.75 to 0.75
- gate_second: bfloat16 [128, 64], replicated, may hold values from -0.5 to 0.5
- teacher: float32 [16, 32768], P(None, ('items', 'events')), may hold values from -12 to 12
Outputs:
- layer_out: bfloat16 [16, 2048, 1024], P('items', 'events')
- scores: float32 [16, 32768], P(None, ('items', 'events'))
- dvalues: float32 [16, 2048, 1024], P('items', 'events')
The draws below stay inside these ranges and needn't reach their ends.
Inputs may be any that keep to these rules, and one draw needn't show every extreme that they name: `lengths`: each user's real events; later positions are padding. `item_codes`: each word holds four codes of 0 to 15, code n of word w being floor(word / 16^n) mod 16, for feature 4 w + n.
All inputs are finite; a program needn't handle non-finite values.
Results may differ from the reference program's by a relative error of at most 0.011.
Values may be sent and summed in bfloat16 or wider, within the bound.
A program may use at most 128 MiB of HBM per device.

```python
import math
import jax
import jax.numpy as jnp
from jax import lax

D = 1024
HEADS = 8
COMPS = 8
ITEM_COMPS = 8
GATE_HID = 128
ACTIONS = 16
LENGTH = 2048
ITEM_DEV = 128
LOGITS = 64
WORDS = 256
B = 16
ITEMS = 32768


def draw_lengths(key, part):
    key = jax.random.fold_in(key, 11)
    key_base, key_first, key_offset = jax.random.split(key, 3)
    base = jax.random.randint(key_base, (B,), LENGTH // 4, LENGTH + 1)
    first_user = jax.random.randint(key_first, (), 0, B)
    offset = jax.random.randint(key_offset, (), 1, B)
    second_user = (first_user + offset) % B
    return base.at[first_user].set(LENGTH).at[second_user].set(LENGTH // 4).astype(jnp.int32)


def with_ends(entries, stream_key, least, top_value):
    place = [jax.random.randint(jax.random.fold_in(stream_key, axis), (), 0, length) for axis, length in enumerate(entries.shape)]
    longest = entries.shape.index(max(entries.shape))
    next_to = place[:longest] + [(place[longest] + 1) % entries.shape[longest]] + place[longest + 1:]
    return entries.at[tuple(place)].set(least).at[tuple(next_to)].set(top_value)


def with_spikes(array, rng, source, target, parts, factor):
    def block_of(position):
        return (jnp.arange(array.shape[position]) // (array.shape[position] // parts)).reshape((-1,) + (1,) * (array.ndim - 1 - position))

    first = jax.random.permutation(rng, parts)[block_of(target)]
    other_side = (block_of(target) + parts // 2) % parts
    return jnp.where((block_of(source) == first) | (block_of(source) == other_side), factor * array, array)


def steps_of(own_key, dims, cuts, least, high):
    def one(position, blocks):
        draws = jax.random.uniform(jax.random.fold_in(jax.random.fold_in(own_key, 6), position), (blocks,), jnp.float32, least / len(cuts), high / len(cuts))
        return jnp.repeat(jnp.exp(draws), dims[position] // blocks).reshape((-1,) + (1,) * (len(dims) - position - 1))

    level = one(*cuts[0])
    for cut in cuts[1:]:
        level = level * one(*cut)
    return level


def scatter_about(own_key, dims, scale, reach, pieces=(), kind=jnp.bfloat16):
    values = scale * jax.random.normal(own_key, dims, jnp.float32)
    if pieces:
        values = values * steps_of(own_key, dims, pieces, -0.22, 0.18)
    return jnp.clip(values, -reach, reach).astype(kind)


def noise_with(key, dims, deviation, most, cuts, heavy, held_as=jnp.bfloat16):
    drawn = deviation * jax.random.normal(key, dims, jnp.float32)
    if cuts:
        drawn = drawn * steps_of(key, dims, cuts, -0.22, 0.18)
    return jnp.clip(with_spikes(drawn, jax.random.fold_in(key, 3), *heavy), -most, most).astype(held_as)


def setup_inputs(seed: int = 0) -> dict:
    key_of = jax.random.split(jax.random.key(seed), 14)
    return {
        "history": scatter_about(key_of[0], (B, LENGTH, D), 1.0, 6.0, ((0, 16), (1, 16))),
        "actions": with_ends(jax.random.randint(key_of[1], (B, LENGTH), 0, ACTIONS), jax.random.fold_in(key_of[1], 1), 0, ACTIONS - 1).astype(jnp.int32),
        "action_table": scatter_about(key_of[2], (ACTIONS, D), 0.5, 3.0),
        "lengths": draw_lengths(jax.random.fold_in(key_of[13], 71), 0),
        "input_gain": jnp.clip(1.0 + 0.15 * jax.random.normal(key_of[4], (D,), jnp.float32), 0.25, 1.75),
        "input_weight": scatter_about(key_of[5], (D, 4 * D), D ** -0.5, 0.1875),
        "output_gain": jnp.clip(1.0 + 0.15 * jax.random.normal(key_of[6], (D,), jnp.float32), 0.25, 1.75),
        "output_weight": scatter_about(key_of[7], (D, D), D ** -0.5, 0.1875),
        "item_codes": with_ends(jax.random.randint(key_of[8], (ITEMS, WORDS), 0, 65536), jax.random.fold_in(key_of[8], 1), 0, 65535).astype(jnp.int32),
        "item_scale": jnp.clip(jnp.exp(math.log(0.06) - 2.3025851 * jax.random.uniform(key_of[9], (ITEMS, ITEM_COMPS), jnp.float32) ** steps_of(key_of[9], (ITEMS, ITEM_COMPS), ((0, 256),), -0.2, 0.2)), 0.006, 0.06),
        "gate_first": scatter_about(key_of[10], (LOGITS, GATE_HID), LOGITS ** -0.5, 0.75),
        "gate_second": scatter_about(key_of[11], (GATE_HID, LOGITS), GATE_HID ** -0.5, 0.5),
        "teacher": noise_with(key_of[12], (B, ITEMS), 2.0, 12.0, ((1, 256),), (1, 0, 16, 2.0), jnp.float32),
    }


epsilon = 1e-05
highest = lax.Precision.HIGHEST

def sigmoid_linear(value_in):
    return value_in * jax.nn.sigmoid(value_in)

def sigmoid_linear_slope(value_in):
    sigmoid_v = jax.nn.sigmoid(value_in)
    return sigmoid_v * (1.0 + value_in * (1.0 - sigmoid_v))

def layer_norm(value_in, gain):
    center = value_in - lax.optimization_barrier(jnp.mean(value_in, axis=-1, keepdims=True))
    spread = lax.rsqrt(lax.optimization_barrier(jnp.mean(center * center, axis=-1, keepdims=True)) + epsilon)
    return center * spread * gain

def dequantize(codes, scales):
    repeated = jnp.repeat(codes, 4, axis=1)
    column = jnp.arange(repeated.shape[1], dtype=jnp.int32)
    powers = (16 ** (column % 4)).astype(jnp.int32)
    nibble = repeated // powers[None, :] % 16
    comp_scale = jnp.repeat(scales, repeated.shape[1] // scales.shape[1], axis=1)
    return ((nibble.astype(jnp.float32) - 7.5) * comp_scale).astype(jnp.bfloat16)

def score_items(user_emb, item_vec, targets, gate_first, gate_second):
    user_count, width = user_emb.shape
    item_count = item_vec.shape[0]
    comp_size = width // COMPS
    user_parts = user_emb.reshape(user_count, COMPS, comp_size).astype(jnp.float32)
    item_parts = item_vec.reshape(item_count, ITEM_COMPS, comp_size).astype(jnp.float32)
    logits = jnp.einsum('bad,tcd->btac', user_parts, item_parts).reshape(user_count, item_count, COMPS * ITEM_COMPS)
    first_w = gate_first.astype(jnp.float32)
    second_w = gate_second.astype(jnp.float32)
    gate_pre = jnp.einsum('btp,pk->btk', logits, first_w, precision=highest)
    gate_hidden = sigmoid_linear(gate_pre)
    gates = jax.nn.sigmoid(jnp.einsum('btk,kp->btp', gate_hidden, second_w, precision=highest))
    scores = lax.optimization_barrier(jnp.sum(gates * logits, axis=-1))
    residual = scores - targets
    slope = gates * (1.0 - gates) * logits
    back_hidden = jnp.einsum('btp,kp->btk', slope, second_w, precision=highest) * sigmoid_linear_slope(gate_pre)
    dlogits = residual[:, :, None] * (gates + jnp.einsum('btk,pk->btp', back_hidden, first_w, precision=highest))
    dembed = jnp.einsum('btac,tcd->bad', dlogits.reshape(user_count, item_count, COMPS, ITEM_COMPS), item_parts, precision=highest)
    return (scores, dembed.reshape(user_count, width))

def reference(history, actions, action_table, lengths, input_gain, input_weight, output_gain, output_weight, item_codes, item_scale, gate_first, gate_second, teacher):
    head_size = D // HEADS
    positions = jnp.arange(LENGTH, dtype=jnp.int32)
    causal = positions[None, :] <= positions[:, None]

    def one_user(inputs):
        user_history, user_actions, user_length = inputs
        onehot = (user_actions[:, None] == jnp.arange(ACTIONS, dtype=jnp.int32)[None, :]).astype(jnp.bfloat16)
        summed = user_history.astype(jnp.float32) + jnp.dot(onehot, action_table, preferred_element_type=jnp.float32)
        normed = layer_norm(summed, input_gain).astype(jnp.bfloat16)
        projection = jnp.dot(normed, input_weight, preferred_element_type=jnp.float32)
        gate_u = sigmoid_linear(projection[:, :D])
        queries = sigmoid_linear(projection[:, D:2 * D]).astype(jnp.bfloat16)
        keys = sigmoid_linear(projection[:, 2 * D:3 * D]).astype(jnp.bfloat16)
        values = sigmoid_linear(projection[:, 3 * D:]).astype(jnp.bfloat16)
        query_heads = queries.reshape(LENGTH, HEADS, head_size).astype(jnp.float32)
        key_heads = keys.reshape(LENGTH, HEADS, head_size).astype(jnp.float32)
        value_heads = values.reshape(LENGTH, HEADS, head_size).astype(jnp.float32)
        raw_scores = jnp.einsum('ihd,jhd->hij', query_heads, key_heads) * head_size ** (-0.5)
        allowed = causal & (positions[None, :] < user_length)
        weights = jnp.where(allowed[None], sigmoid_linear(raw_scores) / LENGTH, 0.0).astype(jnp.bfloat16)
        mixed = jnp.einsum('hij,jhd->ihd', weights.astype(jnp.float32), value_heads).reshape(LENGTH, D)
        gated = (layer_norm(mixed, output_gain) * gate_u).astype(jnp.bfloat16)
        layer_out = (summed + jnp.dot(gated, output_weight, preferred_element_type=jnp.float32)).astype(jnp.bfloat16)
        last_index = (user_length - 1).astype(jnp.int32)
        user_row = lax.dynamic_index_in_dim(layer_out, last_index, 0, keepdims=False)
        mixed_row = lax.dynamic_index_in_dim(mixed, last_index, 0, keepdims=False)
        gate_row = lax.dynamic_index_in_dim(gate_u, last_index, 0, keepdims=False)
        weight_row = lax.dynamic_index_in_dim(weights, last_index, 1, keepdims=False)
        return (layer_out, user_row, mixed_row, gate_row, weight_row)
    layer_out, user_emb, mixed_rows, gate_rows, weight_rows = lax.map(one_user, (history, actions, lengths))
    blocks = ITEMS // ITEM_DEV
    code_blocks = item_codes.reshape(blocks, ITEM_DEV, item_codes.shape[1])
    scale_blocks = item_scale.reshape(blocks, ITEM_DEV, ITEM_COMPS)
    teacher_blocks = jnp.transpose(teacher.reshape(B, blocks, ITEM_DEV), (1, 0, 2))

    def block_step(dembed, inputs):
        codes, scales, targets = inputs
        item_vec = dequantize(codes, scales)
        block_scores, block_grad = score_items(user_emb, item_vec, targets, gate_first, gate_second)
        return (dembed + block_grad, block_scores)
    dembed, score_blocks = lax.scan(block_step, jnp.zeros((B, D), jnp.float32), (code_blocks, scale_blocks, teacher_blocks))
    scores = jnp.transpose(score_blocks, (1, 0, 2)).reshape(B, ITEMS)
    dgated = jnp.dot(dembed.astype(jnp.bfloat16), output_weight.T, preferred_element_type=jnp.float32)
    center = mixed_rows - lax.optimization_barrier(jnp.mean(mixed_rows, axis=-1, keepdims=True))
    spread = lax.rsqrt(lax.optimization_barrier(jnp.mean(center * center, axis=-1, keepdims=True)) + epsilon)
    normal = center * spread
    slope_in = dgated * gate_rows * output_gain
    dmixed = (slope_in - lax.optimization_barrier(jnp.mean(slope_in, axis=-1, keepdims=True)) - normal * lax.optimization_barrier(jnp.mean(slope_in * normal, axis=-1, keepdims=True))) * spread
    weight_cols = jnp.transpose(weight_rows.astype(jnp.float32), (0, 2, 1))
    dvalues = weight_cols[:, :, :, None] * dmixed.reshape(B, 1, HEADS, head_size)
    return (layer_out, scores, dvalues.reshape(B, LENGTH, D))
```

```python
import functools

import jax
import jax.numpy as jnp
from jax import lax
from jax.experimental import pallas as pl
from jax.experimental.pallas import tpu as pltpu
from jax.sharding import PartitionSpec as P

MESH = pl.DeviceIdType.MESH
HEADS = 8
COMPS = 8
ITEM_COMPS = 8
LENGTH = 2048
LANES = 128
EPS = 1e-05
F32, BF16 = jnp.float32, jnp.bfloat16
CHUNK = 512
ORDER = (4, 6, 5, 7, 2, 3, 0, 1)


def dot(a, b, ca=1, cb=0):
    return lax.dot_general(a, b, (((ca,), (cb,)), ((), ())), preferred_element_type=F32)


def silu(v):
    half = 0.5 * v
    return half * jnp.tanh(half) + half


def sigmoid(v):
    return 0.5 * jnp.tanh(0.5 * v) + 0.5


def iota(shape, dim):
    return lax.broadcasted_iota(jnp.int32, shape, dim)


def cols(h):
    return slice(h * LANES, (h + 1) * LANES)


def mean_all(v, count):
    return jnp.sum(jnp.sum(v, axis=1, keepdims=True), axis=0, keepdims=True) * (1.0 / count)


def to_rows(c):
    return jnp.concatenate([jnp.broadcast_to(c[h : h + 1, :], (8, LANES)) for h in range(8)], axis=1)


def to_compact(rows):
    sub = iota((8, LANES), 0)
    out = jnp.zeros((8, LANES), F32)
    for h in range(8):
        out = out + jnp.where(sub == h, rows[:, cols(h)], 0.0)
    return out


def kernel(
    n_items,
    n_events,
    hist_in,
    actions_ref,
    table_in,
    lengths_ref,
    igain_ref,
    igain_c_ref,
    w_in,
    ogain_ref,
    ogain_c_ref,
    wo_in,
    codes_in,
    scale_ref,
    g1_ref,
    g2t_ref,
    teacher_ref,
    layer_ref,
    scores_ref,
    dval_ref,
    hist,
    table,
    codes,
    w,
    wo,
    in_sem,
    w_sem,
    summed,
    lhs,
    gate_u,
    kv_send,
    q_send,
    kv_all,
    q_all,
    mret,
    mixbuf,
    last_src,
    last_buf,
    part_src,
    part_buf,
    user_src,
    user_buf,
    de_src,
    rs_buf,
    ar_src,
    ar_buf,
    lref,
    dref,
    items_t,
    small_send,
    small_recv,
    loc_sem,
    kv_ssem,
    kv_rsem,
    q_ssem,
    q_rsem,
    fwd_ssem,
    fwd_rsem,
    ret_ssem,
    ret_rsem,
):
    i = lax.axis_index("items")
    e = lax.axis_index("events")
    chips = n_events // 2
    my_chip, core = e // 2, e % 2
    sibling = 2 * my_chip + (1 - core)
    rows = hist.shape[0]
    width = hist.shape[1]
    length = lengths_ref[0]

    loads = [
        pltpu.make_async_copy(hist_in.at[0], hist, in_sem.at[0]),
        pltpu.make_async_copy(table_in, table, in_sem.at[1]),
        pltpu.make_async_copy(codes_in, codes, in_sem.at[2]),
        pltpu.make_async_copy(wo_in, wo, in_sem.at[3]),
    ]
    wloads = {
        c: pltpu.make_async_copy(
            w_in.at[:, pl.ds(c * CHUNK, CHUNK)], w.at[c], w_sem.at[c]
        )
        for c in ORDER
    }
    loads[0].start()
    loads[1].start()
    for c in ORDER:
        wloads[c].start()
    loads[2].start()
    loads[3].start()

    barrier = pltpu.get_barrier_semaphore()

    def greet_events(k, _):
        pl.semaphore_signal(
            barrier, inc=1, device_id=(i, lax.rem(e + k, n_events)), device_id_type=MESH
        )
        return 0

    def greet_items(k, _):
        pl.semaphore_signal(
            barrier, inc=1, device_id=(lax.rem(i + k, n_items), e), device_id_type=MESH
        )
        return 0

    lax.fori_loop(1, n_events, greet_events, 0)
    lax.fori_loop(1, n_items, greet_items, 0)

    def to_events(src, buf, phase):
        def go(k, _):
            pltpu.make_async_remote_copy(
                src_ref=src,
                dst_ref=buf.at[k - 1],
                send_sem=small_send.at[phase],
                recv_sem=small_recv.at[phase],
                device_id=(i, lax.rem(e + k, n_events)),
                device_id_type=MESH,
            ).start()
            return 0

        lax.fori_loop(1, n_events, go, 0)

    def small_wait(buf, count, sem):
        part = buf.at[pl.ds(0, count)]
        pltpu.make_async_copy(part, part, sem).wait()

    loads[0].wait()
    loads[1].wait()
    onehot_t = (iota((16, rows), 0) == jnp.broadcast_to(actions_ref[...], (16, rows))).astype(BF16)
    s_val = hist[...].astype(F32) + dot(onehot_t, table[...], 0, 0)
    summed[...] = s_val
    at_last = (iota((rows, LANES), 0) + e * rows) == (length - 1)
    picked = jnp.concatenate(
        [jnp.sum(jnp.where(at_last, s_val[:, cols(h)], 0.0), axis=0, keepdims=True) for h in range(8)],
        axis=0,
    )
    last_src[...] = picked
    center = s_val - jnp.mean(s_val, axis=1, keepdims=True)
    spread = lax.rsqrt(jnp.mean(center * center, axis=1, keepdims=True) + EPS)
    lhs[pl.ds(0, rows), :] = (center * spread * igain_ref[...]).astype(BF16)

    pl.semaphore_wait(barrier, n_events - 1 + n_items - 1)
    to_events(last_src, last_buf, 0)

    normed = lhs[pl.ds(0, rows), :]
    keep_row = (iota((rows, LANES), 0) + e * rows) < length
    for c in (4, 6, 5, 7):
        wloads[c].wait()
        y = silu(dot(normed, w[c]))
        for j in range(CHUNK // LANES):
            head = (c % 2) * (CHUNK // LANES) + j
            block = y[:, cols(j)]
            if c < 6:
                kv_send[head, 0] = block.astype(BF16)
            else:
                kv_send[head, 1] = jnp.where(keep_row, block, 0.0).astype(BF16)

    small_wait(last_buf, n_events - 1, small_recv.at[0])
    summed_c = last_src[...]
    for k in range(n_events - 1):
        summed_c = summed_c + last_buf[k]
    center = summed_c - mean_all(summed_c, width)
    spread = lax.rsqrt(mean_all(center * center, width) + EPS)
    last_rows = to_rows(center * spread * igain_c_ref[...])
    lhs[pl.ds(rows, 16), :] = jnp.concatenate([last_rows, last_rows], axis=0).astype(BF16)

    both = lhs[...]
    sub = iota((8, LANES), 0)
    q_scores = jnp.zeros((8, rows), F32)
    for c in (2, 3):
        wloads[c].wait()
        y = silu(dot(both, w[c]))
        for j in range(CHUNK // LANES):
            head = (c % 2) * (CHUNK // LANES) + j
            q_send[head] = y[:rows, cols(j)].astype(BF16)
            q_diag = jnp.where(sub == head, y[rows : rows + 8, cols(j)], 0.0).astype(BF16)
            q_scores = q_scores + dot(q_diag, kv_send[head, 0], 1, 1)

    inv = width // HEADS
    keep_col = (iota((8, rows), 1) + e * rows) < length
    w_last = jnp.where(keep_col, silu(q_scores * inv ** (-0.5)) * (1.0 / LENGTH), 0.0).astype(BF16)
    part = jnp.zeros((8, LANES), F32)
    for head in range(HEADS):
        part = part + jnp.where(sub == head, dot(w_last, kv_send[head, 1]), 0.0)
    part_src[...] = part
    to_events(part_src, part_buf, 1)

    owner = lax.rem(e + my_chip, 2)

    def kv_copy(k, target_core, block, sem_s, sem_r):
        chip = lax.rem(my_chip + k, chips)
        return pltpu.make_async_remote_copy(
            src_ref=kv_send.at[chip],
            dst_ref=kv_all.at[block],
            send_sem=sem_s,
            recv_sem=sem_r,
            device_id=(i, 2 * chip + target_core),
            device_id_type=MESH,
        )

    own_kv = pltpu.make_async_copy(kv_send.at[my_chip], kv_all.at[e], loc_sem)
    own_kv.start()
    sib_kv = pltpu.make_async_remote_copy(
        src_ref=kv_send.at[my_chip],
        dst_ref=kv_all.at[e],
        send_sem=fwd_ssem,
        recv_sem=fwd_rsem,
        device_id=(i, sibling),
        device_id_type=MESH,
    )
    sib_kv.start()

    def send_kv(k, _):
        kv_copy(k, core, e, kv_ssem, kv_rsem.at[k]).start()
        return 0

    lax.fori_loop(1, chips, send_kv, 0)

    def q_remote(chip):
        return pltpu.make_async_remote_copy(
            src_ref=q_send.at[chip],
            dst_ref=q_all.at[my_chip],
            send_sem=q_ssem,
            recv_sem=q_rsem,
            device_id=(i, 2 * chip + owner),
            device_id_type=MESH,
        )

    def send_q(k, _):
        q_remote(lax.rem(my_chip + k, chips)).start()
        return 0

    lax.fori_loop(1, chips, send_q, 0)

    @pl.when(owner == core)
    def _():
        pltpu.make_async_copy(q_send.at[my_chip], q_all.at[my_chip], q_rsem).start()

    @pl.when(owner != core)
    def _():
        q_remote(my_chip).start()

    gate_rows = []
    for c in (0, 1):
        wloads[c].wait()
        y = silu(dot(both, w[c]))
        gate_u[:, c * CHUNK : (c + 1) * CHUNK] = y[:rows]
        gate_rows.append(y[rows : rows + 8])
    gate_c = to_compact(jnp.concatenate(gate_rows, axis=1))

    loads[2].wait()
    p_i, q_i = iota((512, 512), 0), iota((512, 512), 1)
    expand = jnp.where(p_i == 4 * (q_i & 127) + (q_i >> 7), 1.0, 0.0).astype(BF16)
    for half in range(2):
        words = codes[:, cols(half)]
        nibbles = jnp.concatenate(
            [(((words >> (4 * n)) & 15).astype(F32) - 7.5).astype(BF16) for n in range(4)], axis=1
        )
        raw = dot(expand, nibbles, 1, 1)
        for j in range(4):
            c = half * 4 + j
            items_t[c] = (raw[j * LANES : (j + 1) * LANES] * scale_ref[c : c + 1, :]).astype(BF16)
    logit_count = COMPS * ITEM_COMPS
    r_i, s_i = iota((logit_count, logit_count), 0), iota((logit_count, logit_count), 1)
    perm = jnp.where(s_i == (r_i & 7) * 8 + (r_i >> 3), 1.0, 0.0).astype(BF16)
    g1, g2t = g1_ref[...], g2t_ref[...]
    m_first_t = dot(g1, perm, 0, 1).astype(BF16)
    m_first = dot(perm, g1).astype(BF16)
    m_second_t = dot(perm, g2t).astype(BF16)
    m_second = dot(g2t, perm, 0, 1).astype(BF16)

    small_wait(part_buf, n_events - 1, small_recv.at[1])
    mixed_c = part_src[...]
    for k in range(n_events - 1):
        mixed_c = mixed_c + part_buf[k]
    center_c = mixed_c - mean_all(mixed_c, width)
    spread_c = lax.rsqrt(mean_all(center_c * center_c, width) + EPS)
    normal_c = center_c * spread_c
    gated_c = normal_c * ogain_c_ref[...] * gate_c
    loads[3].wait()
    user_rows = dot(to_rows(gated_c).astype(BF16), wo[...])
    user_c = (summed_c + to_compact(user_rows)).astype(BF16).astype(F32)
    user_src[...] = user_c
    user_buf[i] = user_c

    def send_user(k, _):
        pltpu.make_async_remote_copy(
            src_ref=user_src,
            dst_ref=user_buf.at[i],
            send_sem=small_send.at[2],
            recv_sem=small_recv.at[2],
            device_id=(lax.rem(i + k, n_items), e),
            device_id_type=MESH,
        ).start()
        return 0

    lax.fori_loop(1, n_items, send_user, 0)

    users = n_items
    small_wait(user_buf, n_items - 1, small_recv.at[2])
    everyone = user_buf[...].reshape(users * 8, LANES).astype(BF16)
    for c in range(ITEM_COMPS):
        part_l = dot(everyone, items_t[c])
        for b in range(users):
            lref[c * 8 : (c + 1) * 8, cols(b)] = part_l[b * 8 : (b + 1) * 8]
    for b0 in range(0, users, 2):
        span = slice(b0 * LANES, (b0 + 2) * LANES)
        logits = lref[:, span]
        pre = dot(m_first_t, logits.astype(BF16))
        sig = sigmoid(pre)
        gates = sigmoid(dot(m_second_t, (pre * sig).astype(BF16)))
        gl = gates * logits
        score = jnp.sum(gl, axis=0, keepdims=True)
        targets = jnp.concatenate(
            [teacher_ref[b0 : b0 + 1, :], teacher_ref[b0 + 1 : b0 + 2, :]], axis=1
        )
        scores_ref[b0 : b0 + 1, :] = score[:, :LANES]
        scores_ref[b0 + 1 : b0 + 2, :] = score[:, LANES:]
        slope = (gl * (1.0 - gates)).astype(BF16)
        back = dot(m_second, slope) * (sig * (1.0 + pre * (1.0 - sig)))
        dlog = (score - targets) * (gates + dot(m_first, back.astype(BF16)))
        for c in range(ITEM_COMPS):
            for j in range(2):
                b = b0 + j
                dref[c, b * 8 : (b + 1) * 8, :] = dlog[c * 8 : (c + 1) * 8, cols(j)]
    demb = jnp.zeros((users * 8, LANES), F32)
    for c in range(ITEM_COMPS):
        demb = demb + dot(dref[c].astype(BF16), items_t[c], 1, 1)
    de_src[...] = demb.reshape(users, 8, LANES)

    def send_de(k, _):
        other = lax.rem(i + k, n_items)
        pltpu.make_async_remote_copy(
            src_ref=de_src.at[other],
            dst_ref=rs_buf.at[k - 1],
            send_sem=small_send.at[3],
            recv_sem=small_recv.at[3],
            device_id=(other, e),
            device_id_type=MESH,
        ).start()
        return 0

    lax.fori_loop(1, n_items, send_de, 0)

    own_kv.wait()

    def forward(k, _):
        source = 2 * lax.rem(my_chip + chips - k, chips) + core
        pltpu.make_async_copy(kv_all.at[source], kv_all.at[source], kv_rsem.at[k]).wait()
        pltpu.make_async_remote_copy(
            src_ref=kv_all.at[source],
            dst_ref=kv_all.at[source],
            send_sem=fwd_ssem,
            recv_sem=fwd_rsem,
            device_id=(i, sibling),
            device_id_type=MESH,
        ).start()
        return 0

    lax.fori_loop(1, chips, forward, 0)

    small_wait(rs_buf, n_items - 1, small_recv.at[3])
    red = de_src[i]
    for k in range(n_items - 1):
        red = red + rs_buf[k]
    ar_src[...] = red
    to_events(ar_src, ar_buf, 4)

    half_blocks = kv_all.at[pl.ds(0, chips)]
    pltpu.make_async_copy(half_blocks, half_blocks, fwd_rsem).wait()
    pltpu.make_async_copy(q_all, q_all, q_rsem).wait()
    half_scale = 0.5 * inv ** (-0.5)
    for n in range(chips):
        query = q_all[n]
        odd = lax.rem(core + n, 2)
        acc = jnp.zeros((rows, LANES), F32)
        for m in range(n + 1):
            key = jnp.concatenate([kv_all[2 * m, 0], kv_all[2 * m + 1, 0]], axis=0)
            value = jnp.concatenate([kv_all[2 * m, 1], kv_all[2 * m + 1, 1]], axis=0)
            half = dot(query, key, 1, 1) * half_scale
            weight = half * jnp.tanh(half) + half
            if m == n:
                causal = iota((rows, 2 * rows), 1) <= iota((rows, 2 * rows), 0) + odd * rows
                weight = jnp.where(causal, weight, 0.0)
            acc = acc + dot(weight.astype(BF16), value)
        mret[n] = acc

    def ret_remote(n, target):
        return pltpu.make_async_remote_copy(
            src_ref=mret.at[n],
            dst_ref=mixbuf.at[my_chip],
            send_sem=ret_ssem,
            recv_sem=ret_rsem,
            device_id=(i, target),
            device_id_type=MESH,
        )

    def ret_target(n):
        return 2 * n + lax.rem(n + core, 2)

    def send_ret(n, _):
        target = ret_target(n)

        @pl.when(target == e)
        def _():
            pltpu.make_async_copy(mret.at[n], mixbuf.at[my_chip], ret_rsem).start()

        @pl.when(target != e)
        def _():
            ret_remote(n, target).start()

        return 0

    lax.fori_loop(0, chips, send_ret, 0)

    small_wait(ar_buf, n_events - 1, small_recv.at[4])
    total = ar_src[...]
    for k in range(n_events - 1):
        total = total + ar_buf[k]
    dgated = to_compact(dot(to_rows(total).astype(BF16), wo[...], 1, 1))
    s_c = dgated * gate_c * ogain_c_ref[...]
    dmixed = (
        s_c - mean_all(s_c, width) - normal_c * mean_all(s_c * normal_c, width)
    ) * spread_c
    diag = jnp.concatenate([jnp.where(sub == h, dmixed, 0.0) for h in range(8)], axis=1)
    hi = diag.astype(BF16)
    lo = (diag - hi.astype(F32)).astype(BF16)
    w2 = jnp.concatenate([w_last.astype(F32), w_last.astype(F32)], axis=0).astype(BF16)
    hilo = jnp.concatenate([hi.astype(F32), lo.astype(F32)], axis=0).astype(BF16)
    dval_ref[0] = dot(w2, hilo, 0, 0)

    pltpu.make_async_copy(mixbuf, mixbuf, ret_rsem).wait()
    scale = 1.0 / LENGTH
    tot = jnp.zeros((rows, 1), F32)
    for h in range(HEADS):
        tot = tot + jnp.sum(mixbuf[h], axis=1, keepdims=True)
    mean = tot * (1.0 / width)
    var = jnp.zeros((rows, 1), F32)
    for h in range(HEADS):
        c_h = (mixbuf[h] - mean) * scale
        var = var + jnp.sum(c_h * c_h, axis=1, keepdims=True)
    spread = lax.rsqrt(var * (1.0 / width) + EPS) * scale
    gated = jnp.concatenate(
        [
            ((mixbuf[h] - mean) * spread * ogain_ref[:, cols(h)] * gate_u[:, cols(h)]).astype(BF16)
            for h in range(HEADS)
        ],
        axis=1,
    )
    layer_ref[0] = (summed[...] + dot(gated, wo[...])).astype(BF16)

    small_wait(last_buf, n_events - 1, small_send.at[0])
    small_wait(part_buf, n_events - 1, small_send.at[1])
    small_wait(user_buf, n_items - 1, small_send.at[2])
    small_wait(rs_buf, n_items - 1, small_send.at[3])
    small_wait(ar_buf, n_events - 1, small_send.at[4])
    kv_part = kv_send.at[pl.ds(0, chips - 1)]
    pltpu.make_async_copy(kv_part, kv_part, kv_ssem).wait()
    pltpu.make_async_copy(kv_send, kv_send, fwd_ssem).wait()
    q_part = q_send.at[pl.ds(0, chips - 1)]
    pltpu.make_async_copy(q_part, q_part, q_ssem).wait()

    @pl.when(owner != core)
    def _():
        q_remote(my_chip).wait_send()

    def ret_wait(n, _):
        target = ret_target(n)

        @pl.when(target != e)
        def _():
            ret_remote(n, target).wait_send()

        return 0

    lax.fori_loop(0, chips, ret_wait, 0)


def local(
    n_items,
    n_events,
    history,
    actions,
    action_table,
    lengths,
    input_gain,
    input_weight,
    output_gain,
    output_weight,
    item_codes,
    item_scale,
    gate_first,
    gate_second,
    teacher,
):
    _, rows, width = history.shape
    chips = n_events // 2
    items = item_codes.shape[0]
    users = n_items
    small = (8, LANES)
    vmem = pl.BlockSpec(memory_space=pltpu.VMEM)
    smem = pl.BlockSpec(memory_space=pltpu.SMEM)
    hbm = pl.BlockSpec(memory_space=pl.ANY)
    dma = pltpu.SemaphoreType.DMA
    layer, scores, dvalues = pl.pallas_call(
        functools.partial(kernel, n_items, n_events),
        out_shape=(
            jax.ShapeDtypeStruct((1, rows, width), BF16),
            jax.ShapeDtypeStruct((users, items), F32),
            jax.ShapeDtypeStruct((1, rows, width), F32),
        ),
        in_specs=[hbm, vmem, hbm, smem, vmem, vmem, hbm, vmem, vmem, hbm, hbm, vmem, vmem, vmem, vmem],
        out_specs=(vmem, vmem, vmem),
        scratch_shapes=[
            pltpu.VMEM((rows, width), BF16),
            pltpu.VMEM(action_table.shape, BF16),
            pltpu.VMEM(item_codes.shape, jnp.int32),
            pltpu.VMEM((4 * width // CHUNK, width, CHUNK), BF16),
            pltpu.VMEM((width, width), BF16),
            dma((4,)),
            dma((4 * width // CHUNK,)),
            pltpu.VMEM((rows, width), F32),
            pltpu.VMEM((rows + 16, width), BF16),
            pltpu.VMEM((rows, width), F32),
            pltpu.VMEM((HEADS, 2, rows, LANES), BF16),
            pltpu.VMEM((HEADS, rows, LANES), BF16),
            pltpu.VMEM((n_events, 2, rows, LANES), BF16),
            pltpu.VMEM((chips, rows, LANES), BF16),
            pltpu.VMEM((chips, rows, LANES), F32),
            pltpu.VMEM((HEADS, rows, LANES), F32),
            pltpu.VMEM(small, F32),
            pltpu.VMEM((n_events - 1,) + small, F32),
            pltpu.VMEM(small, F32),
            pltpu.VMEM((n_events - 1,) + small, F32),
            pltpu.VMEM(small, F32),
            pltpu.VMEM((n_items,) + small, F32),
            pltpu.VMEM((n_items,) + small, F32),
            pltpu.VMEM((n_items - 1,) + small, F32),
            pltpu.VMEM(small, F32),
            pltpu.VMEM((n_events - 1,) + small, F32),
            pltpu.VMEM((COMPS * ITEM_COMPS, users * LANES), F32),
            pltpu.VMEM((ITEM_COMPS, users * 8, LANES), F32),
            pltpu.VMEM((ITEM_COMPS, LANES, items), BF16),
            dma((5,)),
            dma((5,)),
            dma(()),
            dma(()),
            dma((chips,)),
            dma(()),
            dma(()),
            dma(()),
            dma(()),
            dma(()),
            dma(()),
        ],
        compiler_params=pltpu.CompilerParams(
            collective_id=0, has_side_effects=True, vmem_limit_bytes=50 * 1024 * 1024
        ),
    )(
        history,
        actions,
        action_table,
        lengths,
        input_gain.reshape(1, width),
        input_gain.reshape(8, LANES),
        input_weight,
        output_gain.reshape(1, width),
        output_gain.reshape(8, LANES),
        output_weight,
        item_codes,
        item_scale.T,
        gate_first,
        gate_second.T,
        teacher,
    )
    return layer, scores, dvalues


def solution(mesh):
    in_specs = (
        P("items", "events", None),
        P("items", "events"),
        P(),
        P("items"),
        P(),
        P(),
        P(),
        P(),
        P(("items", "events"), None),
        P(("items", "events"), None),
        P(),
        P(),
        P(None, ("items", "events")),
    )
    out_specs = (
        P("items", "events", None),
        P(None, ("items", "events")),
        P("items", "events", None),
    )
    body = functools.partial(local, mesh.shape["items"], mesh.shape["events"])
    return jax.shard_map(body, mesh=mesh, in_specs=in_specs, out_specs=out_specs, check_vma=False)
```

```python
import functools

import jax
import jax.numpy as jnp
from jax import lax
from jax.experimental import pallas as pl
from jax.experimental.pallas import tpu as pltpu
from jax.sharding import PartitionSpec as P

MESH = pl.DeviceIdType.MESH
HEADS = 8
COMPS = 8
ITEM_COMPS = 8
LENGTH = 2048
LANES = 128
EPS = 1e-05
F32, BF16 = jnp.float32, jnp.bfloat16
CHUNK = 512
VMEM_LIMIT = 64 * 1000 * 1000
ORDER = (4, 6, 5, 7, 2, 3, 0, 1)


def dot(a, b, ca=1, cb=0):
    return lax.dot_general(a, b, (((ca,), (cb,)), ((), ())), preferred_element_type=F32)


def silu(v):
    half = 0.5 * v
    return half * jnp.tanh(half) + half


def sigmoid(v):
    return 0.5 * jnp.tanh(0.5 * v) + 0.5


def iota(shape, dim):
    return lax.broadcasted_iota(jnp.int32, shape, dim)


def cols(h):
    return slice(h * LANES, (h + 1) * LANES)


def mean_all(v, count):
    return jnp.sum(jnp.sum(v, axis=1, keepdims=True), axis=0, keepdims=True) * (1.0 / count)


def to_rows(c):
    return jnp.concatenate([jnp.broadcast_to(c[h : h + 1, :], (8, LANES)) for h in range(8)], axis=1)


def to_compact(rows):
    sub = iota((8, LANES), 0)
    out = jnp.zeros((8, LANES), F32)
    for h in range(8):
        out = out + jnp.where(sub == h, rows[:, cols(h)], 0.0)
    return out


def kernel(
    n_items,
    n_events,
    lengths_ref,
    hist_in,
    actions_in,
    table_in,
    igain_in,
    igain_c_in,
    ogain_in,
    ogain_c_in,
    scale_in,
    g1_in,
    g2t_in,
    teacher_in,
    codes_in,
    wo_in,
    w_in,
    layer_out,
    scores_out,
    dval_out,
    hist,
    actions_ref,
    table,
    igain_ref,
    igain_c_ref,
    ogain_ref,
    ogain_c_ref,
    scale_ref,
    g1_ref,
    g2t_ref,
    teacher_ref,
    codes,
    wo,
    w,
    layer_ref,
    scores_ref,
    dval_ref,
    out_sem,
    in_sem,
    w_sem,
    summed,
    lhs,
    gate_u,
    kv_send,
    q_send,
    kv_all,
    q_all,
    mret,
    mixbuf,
    last_src,
    last_buf,
    part_src,
    part_buf,
    user_src,
    user_buf,
    de_src,
    rs_buf,
    ar_src,
    ar_buf,
    lref,
    dref,
    items_t,
    small_send,
    small_recv,
    loc_sem,
    kv_ssem,
    kv_rsem,
    q_ssem,
    q_rsem,
    fwd_ssem,
    fwd_rsem,
    ret_ssem,
    ret_rsem,
):
    i = lax.axis_index("items")
    e = lax.axis_index("events")
    chips = n_events // 2
    my_chip, core = e // 2, e % 2
    sibling = 2 * my_chip + (1 - core)
    rows = hist.shape[0]
    width = hist.shape[1]
    length = lengths_ref[0]

    pairs = (
        (hist_in.at[0], hist),
        (actions_in, actions_ref),
        (table_in, table),
        (igain_in, igain_ref),
        (igain_c_in, igain_c_ref),
        (ogain_in, ogain_ref),
        (ogain_c_in, ogain_c_ref),
        (scale_in, scale_ref),
        (g1_in, g1_ref),
        (g2t_in, g2t_ref),
        (teacher_in, teacher_ref),
        (codes_in, codes),
        (wo_in, wo),
    )
    loads = [pltpu.make_async_copy(a, b, in_sem.at[k]) for k, (a, b) in enumerate(pairs)]
    wloads = {
        c: pltpu.make_async_copy(
            w_in.at[:, pl.ds(c * CHUNK, CHUNK)], w.at[c], w_sem.at[c]
        )
        for c in ORDER
    }
    for k in range(5):
        loads[k].start()
    for c in ORDER:
        wloads[c].start()
    for k in range(5, 13):
        loads[k].start()

    barrier = pltpu.get_barrier_semaphore()

    def greet_events(k, _):
        pl.semaphore_signal(
            barrier, inc=1, device_id=(i, lax.rem(e + k, n_events)), device_id_type=MESH
        )
        return 0

    def greet_items(k, _):
        pl.semaphore_signal(
            barrier, inc=1, device_id=(lax.rem(i + k, n_items), e), device_id_type=MESH
        )
        return 0

    lax.fori_loop(1, n_events, greet_events, 0)
    lax.fori_loop(1, n_items, greet_items, 0)

    def to_events(src, buf, phase):
        def go(k, _):
            pltpu.make_async_remote_copy(
                src_ref=src,
                dst_ref=buf.at[k - 1],
                send_sem=small_send.at[phase],
                recv_sem=small_recv.at[phase],
                device_id=(i, lax.rem(e + k, n_events)),
                device_id_type=MESH,
            ).start()
            return 0

        lax.fori_loop(1, n_events, go, 0)

    def small_wait(buf, count, sem):
        part = buf.at[pl.ds(0, count)]
        pltpu.make_async_copy(part, part, sem).wait()

    for k in range(5):
        loads[k].wait()
    onehot_t = (iota((16, rows), 0) == jnp.broadcast_to(actions_ref[...], (16, rows))).astype(BF16)
    s_val = hist[...].astype(F32) + dot(onehot_t, table[...], 0, 0)
    summed[...] = s_val
    at_last = (iota((rows, LANES), 0) + e * rows) == (length - 1)
    picked = jnp.concatenate(
        [jnp.sum(jnp.where(at_last, s_val[:, cols(h)], 0.0), axis=0, keepdims=True) for h in range(8)],
        axis=0,
    )
    last_src[...] = picked
    center = s_val - jnp.mean(s_val, axis=1, keepdims=True)
    spread = lax.rsqrt(jnp.mean(center * center, axis=1, keepdims=True) + EPS)
    lhs[pl.ds(0, rows), :] = (center * spread * igain_ref[...]).astype(BF16)

    pl.semaphore_wait(barrier, n_events - 1 + n_items - 1)
    to_events(last_src, last_buf, 0)

    normed = lhs[pl.ds(0, rows), :]
    keep_row = (iota((rows, LANES), 0) + e * rows) < length
    for c in (4, 6, 5, 7):
        wloads[c].wait()
        y = silu(dot(normed, w[c]))
        for j in range(CHUNK // LANES):
            head = (c % 2) * (CHUNK // LANES) + j
            block = y[:, cols(j)]
            if c < 6:
                kv_send[head, 0] = block.astype(BF16)
            else:
                kv_send[head, 1] = jnp.where(keep_row, block, 0.0).astype(BF16)

    small_wait(last_buf, n_events - 1, small_recv.at[0])
    summed_c = last_src[...]
    for k in range(n_events - 1):
        summed_c = summed_c + last_buf[k]
    center = summed_c - mean_all(summed_c, width)
    spread = lax.rsqrt(mean_all(center * center, width) + EPS)
    last_rows = to_rows(center * spread * igain_c_ref[...])
    lhs[pl.ds(rows, 16), :] = jnp.concatenate([last_rows, last_rows], axis=0).astype(BF16)

    both = lhs[...]
    sub = iota((8, LANES), 0)
    q_scores = jnp.zeros((8, rows), F32)
    for c in (2, 3):
        wloads[c].wait()
        y = silu(dot(both, w[c]))
        for j in range(CHUNK // LANES):
            head = (c % 2) * (CHUNK // LANES) + j
            q_send[head] = y[:rows, cols(j)].astype(BF16)
            q_diag = jnp.where(sub == head, y[rows : rows + 8, cols(j)], 0.0).astype(BF16)
            q_scores = q_scores + dot(q_diag, kv_send[head, 0], 1, 1)

    inv = width // HEADS
    keep_col = (iota((8, rows), 1) + e * rows) < length
    w_last = jnp.where(keep_col, silu(q_scores * inv ** (-0.5)) * (1.0 / LENGTH), 0.0).astype(BF16)
    part = jnp.zeros((8, LANES), F32)
    for head in range(HEADS):
        part = part + jnp.where(sub == head, dot(w_last, kv_send[head, 1]), 0.0)
    part_src[...] = part
    to_events(part_src, part_buf, 1)

    owner = lax.rem(e + my_chip, 2)

    def kv_copy(k, target_core, block, sem_s, sem_r):
        chip = lax.rem(my_chip + k, chips)
        return pltpu.make_async_remote_copy(
            src_ref=kv_send.at[chip],
            dst_ref=kv_all.at[block],
            send_sem=sem_s,
            recv_sem=sem_r,
            device_id=(i, 2 * chip + target_core),
            device_id_type=MESH,
        )

    own_kv = pltpu.make_async_copy(kv_send.at[my_chip], kv_all.at[e], loc_sem)
    own_kv.start()
    sib_kv = pltpu.make_async_remote_copy(
        src_ref=kv_send.at[my_chip],
        dst_ref=kv_all.at[e],
        send_sem=fwd_ssem,
        recv_sem=fwd_rsem,
        device_id=(i, sibling),
        device_id_type=MESH,
    )
    sib_kv.start()

    def send_kv(k, _):
        kv_copy(k, core, e, kv_ssem, kv_rsem.at[k]).start()
        return 0

    lax.fori_loop(1, chips, send_kv, 0)

    def q_remote(chip):
        return pltpu.make_async_remote_copy(
            src_ref=q_send.at[chip],
            dst_ref=q_all.at[my_chip],
            send_sem=q_ssem,
            recv_sem=q_rsem,
            device_id=(i, 2 * chip + owner),
            device_id_type=MESH,
        )

    def send_q(k, _):
        q_remote(lax.rem(my_chip + k, chips)).start()
        return 0

    lax.fori_loop(1, chips, send_q, 0)

    @pl.when(owner == core)
    def _():
        pltpu.make_async_copy(q_send.at[my_chip], q_all.at[my_chip], q_rsem).start()

    @pl.when(owner != core)
    def _():
        q_remote(my_chip).start()

    gate_rows = []
    for c in (0, 1):
        wloads[c].wait()
        y = silu(dot(both, w[c]))
        gate_u[:, c * CHUNK : (c + 1) * CHUNK] = y[:rows]
        gate_rows.append(y[rows : rows + 8])
    gate_c = to_compact(jnp.concatenate(gate_rows, axis=1))

    for k in range(5, 12):
        loads[k].wait()
    p_i, q_i = iota((512, 512), 0), iota((512, 512), 1)
    expand = jnp.where(p_i == 4 * (q_i & 127) + (q_i >> 7), 1.0, 0.0).astype(BF16)
    for half in range(2):
        words = codes[:, cols(half)]
        nibbles = jnp.concatenate(
            [(((words >> (4 * n)) & 15).astype(F32) - 7.5).astype(BF16) for n in range(4)], axis=1
        )
        raw = dot(expand, nibbles, 1, 1)
        for j in range(4):
            c = half * 4 + j
            items_t[c] = (raw[j * LANES : (j + 1) * LANES] * scale_ref[c : c + 1, :]).astype(BF16)
    logit_count = COMPS * ITEM_COMPS
    r_i, s_i = iota((logit_count, logit_count), 0), iota((logit_count, logit_count), 1)
    perm = jnp.where(s_i == (r_i & 7) * 8 + (r_i >> 3), 1.0, 0.0).astype(BF16)
    g1, g2t = g1_ref[...], g2t_ref[...]
    m_first_t = dot(g1, perm, 0, 1).astype(BF16)
    m_first = dot(perm, g1).astype(BF16)
    m_second_t = dot(perm, g2t).astype(BF16)
    m_second = dot(g2t, perm, 0, 1).astype(BF16)

    small_wait(part_buf, n_events - 1, small_recv.at[1])
    mixed_c = part_src[...]
    for k in range(n_events - 1):
        mixed_c = mixed_c + part_buf[k]
    center_c = mixed_c - mean_all(mixed_c, width)
    spread_c = lax.rsqrt(mean_all(center_c * center_c, width) + EPS)
    normal_c = center_c * spread_c
    gated_c = normal_c * ogain_c_ref[...] * gate_c
    loads[12].wait()
    user_rows = dot(to_rows(gated_c).astype(BF16), wo[...])
    user_c = (summed_c + to_compact(user_rows)).astype(BF16).astype(F32)
    user_src[...] = user_c
    user_buf[i] = user_c

    def send_user(k, _):
        pltpu.make_async_remote_copy(
            src_ref=user_src,
            dst_ref=user_buf.at[i],
            send_sem=small_send.at[2],
            recv_sem=small_recv.at[2],
            device_id=(lax.rem(i + k, n_items), e),
            device_id_type=MESH,
        ).start()
        return 0

    lax.fori_loop(1, n_items, send_user, 0)

    users = n_items
    small_wait(user_buf, n_items - 1, small_recv.at[2])
    everyone = user_buf[...].reshape(users * 8, LANES).astype(BF16)
    for c in range(ITEM_COMPS):
        part_l = dot(everyone, items_t[c])
        for b in range(users):
            lref[c * 8 : (c + 1) * 8, cols(b)] = part_l[b * 8 : (b + 1) * 8]
    for b0 in range(0, users, 2):
        span = slice(b0 * LANES, (b0 + 2) * LANES)
        logits = lref[:, span]
        pre = dot(m_first_t, logits.astype(BF16))
        sig = sigmoid(pre)
        gates = sigmoid(dot(m_second_t, (pre * sig).astype(BF16)))
        gl = gates * logits
        score = jnp.sum(gl, axis=0, keepdims=True)
        targets = jnp.concatenate(
            [teacher_ref[b0 : b0 + 1, :], teacher_ref[b0 + 1 : b0 + 2, :]], axis=1
        )
        scores_ref[b0 : b0 + 1, :] = score[:, :LANES]
        scores_ref[b0 + 1 : b0 + 2, :] = score[:, LANES:]
        slope = (gl * (1.0 - gates)).astype(BF16)
        back = dot(m_second, slope) * (sig * (1.0 + pre * (1.0 - sig)))
        dlog = (score - targets) * (gates + dot(m_first, back.astype(BF16)))
        for c in range(ITEM_COMPS):
            for j in range(2):
                b = b0 + j
                dref[c, b * 8 : (b + 1) * 8, :] = dlog[c * 8 : (c + 1) * 8, cols(j)]
    demb = jnp.zeros((users * 8, LANES), F32)
    for c in range(ITEM_COMPS):
        demb = demb + dot(dref[c].astype(BF16), items_t[c], 1, 1)
    de_src[...] = demb.reshape(users, 8, LANES)

    def send_de(k, _):
        other = lax.rem(i + k, n_items)
        pltpu.make_async_remote_copy(
            src_ref=de_src.at[other],
            dst_ref=rs_buf.at[k - 1],
            send_sem=small_send.at[3],
            recv_sem=small_recv.at[3],
            device_id=(other, e),
            device_id_type=MESH,
        ).start()
        return 0

    lax.fori_loop(1, n_items, send_de, 0)

    out_scores = pltpu.make_async_copy(scores_ref, scores_out, out_sem.at[1])
    out_scores.start()

    own_kv.wait()

    def forward(k, _):
        source = 2 * lax.rem(my_chip + chips - k, chips) + core
        pltpu.make_async_copy(kv_all.at[source], kv_all.at[source], kv_rsem.at[k]).wait()
        pltpu.make_async_remote_copy(
            src_ref=kv_all.at[source],
            dst_ref=kv_all.at[source],
            send_sem=fwd_ssem,
            recv_sem=fwd_rsem,
            device_id=(i, sibling),
            device_id_type=MESH,
        ).start()
        return 0

    lax.fori_loop(1, chips, forward, 0)

    small_wait(rs_buf, n_items - 1, small_recv.at[3])
    red = de_src[i]
    for k in range(n_items - 1):
        red = red + rs_buf[k]
    ar_src[...] = red
    to_events(ar_src, ar_buf, 4)

    half_blocks = kv_all.at[pl.ds(0, chips)]
    pltpu.make_async_copy(half_blocks, half_blocks, fwd_rsem).wait()
    pltpu.make_async_copy(q_all, q_all, q_rsem).wait()
    half_scale = 0.5 * inv ** (-0.5)
    for n in range(chips):
        query = q_all[n]
        odd = lax.rem(core + n, 2)
        acc = jnp.zeros((rows, LANES), F32)
        for m in range(n + 1):
            key = jnp.concatenate([kv_all[2 * m, 0], kv_all[2 * m + 1, 0]], axis=0)
            value = jnp.concatenate([kv_all[2 * m, 1], kv_all[2 * m + 1, 1]], axis=0)
            half = dot(query, key, 1, 1) * half_scale
            weight = half * jnp.tanh(half) + half
            if m == n:
                causal = iota((rows, 2 * rows), 1) <= iota((rows, 2 * rows), 0) + odd * rows
                weight = jnp.where(causal, weight, 0.0)
            acc = acc + dot(weight.astype(BF16), value)
        mret[n] = acc

    def ret_remote(n, target):
        return pltpu.make_async_remote_copy(
            src_ref=mret.at[n],
            dst_ref=mixbuf.at[my_chip],
            send_sem=ret_ssem,
            recv_sem=ret_rsem,
            device_id=(i, target),
            device_id_type=MESH,
        )

    def ret_target(n):
        return 2 * n + lax.rem(n + core, 2)

    def send_ret(n, _):
        target = ret_target(n)

        @pl.when(target == e)
        def _():
            pltpu.make_async_copy(mret.at[n], mixbuf.at[my_chip], ret_rsem).start()

        @pl.when(target != e)
        def _():
            ret_remote(n, target).start()

        return 0

    lax.fori_loop(0, chips, send_ret, 0)

    small_wait(ar_buf, n_events - 1, small_recv.at[4])
    total = ar_src[...]
    for k in range(n_events - 1):
        total = total + ar_buf[k]
    dgated = to_compact(dot(to_rows(total).astype(BF16), wo[...], 1, 1))
    s_c = dgated * gate_c * ogain_c_ref[...]
    dmixed = (
        s_c - mean_all(s_c, width) - normal_c * mean_all(s_c * normal_c, width)
    ) * spread_c
    diag = jnp.concatenate([jnp.where(sub == h, dmixed, 0.0) for h in range(8)], axis=1)
    hi = diag.astype(BF16)
    lo = (diag - hi.astype(F32)).astype(BF16)
    w2 = jnp.concatenate([w_last.astype(F32), w_last.astype(F32)], axis=0).astype(BF16)
    hilo = jnp.concatenate([hi.astype(F32), lo.astype(F32)], axis=0).astype(BF16)
    dval_ref[...] = dot(w2, hilo, 0, 0)

    out_dval = pltpu.make_async_copy(dval_ref, dval_out.at[0], out_sem.at[2])
    out_dval.start()

    pltpu.make_async_copy(mixbuf, mixbuf, ret_rsem).wait()
    scale = 1.0 / LENGTH
    tot = jnp.zeros((rows, 1), F32)
    for h in range(HEADS):
        tot = tot + jnp.sum(mixbuf[h], axis=1, keepdims=True)
    mean = tot * (1.0 / width)
    var = jnp.zeros((rows, 1), F32)
    for h in range(HEADS):
        c_h = (mixbuf[h] - mean) * scale
        var = var + jnp.sum(c_h * c_h, axis=1, keepdims=True)
    spread = lax.rsqrt(var * (1.0 / width) + EPS) * scale
    gated = jnp.concatenate(
        [
            ((mixbuf[h] - mean) * spread * ogain_ref[:, cols(h)] * gate_u[:, cols(h)]).astype(BF16)
            for h in range(HEADS)
        ],
        axis=1,
    )
    layer_ref[...] = (summed[...] + dot(gated, wo[...])).astype(BF16)

    out_layer = pltpu.make_async_copy(layer_ref, layer_out.at[0], out_sem.at[0])
    out_layer.start()

    small_wait(last_buf, n_events - 1, small_send.at[0])
    small_wait(part_buf, n_events - 1, small_send.at[1])
    small_wait(user_buf, n_items - 1, small_send.at[2])
    small_wait(rs_buf, n_items - 1, small_send.at[3])
    small_wait(ar_buf, n_events - 1, small_send.at[4])
    kv_part = kv_send.at[pl.ds(0, chips - 1)]
    pltpu.make_async_copy(kv_part, kv_part, kv_ssem).wait()
    pltpu.make_async_copy(kv_send, kv_send, fwd_ssem).wait()
    q_part = q_send.at[pl.ds(0, chips - 1)]
    pltpu.make_async_copy(q_part, q_part, q_ssem).wait()

    @pl.when(owner != core)
    def _():
        q_remote(my_chip).wait_send()

    def ret_wait(n, _):
        target = ret_target(n)

        @pl.when(target != e)
        def _():
            ret_remote(n, target).wait_send()

        return 0

    lax.fori_loop(0, chips, ret_wait, 0)
    out_scores.wait()
    out_dval.wait()
    out_layer.wait()


def local(
    n_items,
    n_events,
    history,
    actions,
    action_table,
    lengths,
    input_gain,
    input_weight,
    output_gain,
    output_weight,
    item_codes,
    item_scale,
    gate_first,
    gate_second,
    teacher,
):
    _, rows, width = history.shape
    chips = n_events // 2
    items = item_codes.shape[0]
    users = n_items
    small = (8, LANES)
    smem = pl.BlockSpec(memory_space=pltpu.SMEM)
    hbm = pl.BlockSpec(memory_space=pl.ANY)
    dma = pltpu.SemaphoreType.DMA
    layer, scores, dvalues = pl.pallas_call(
        functools.partial(kernel, n_items, n_events),
        out_shape=(
            jax.ShapeDtypeStruct((1, rows, width), BF16),
            jax.ShapeDtypeStruct((users, items), F32),
            jax.ShapeDtypeStruct((1, rows, width), F32),
        ),
        in_specs=[smem] + [hbm] * 14,
        out_specs=(hbm, hbm, hbm),
        scratch_shapes=[
            pltpu.VMEM((rows, width), BF16),
            pltpu.VMEM(actions.shape, jnp.int32),
            pltpu.VMEM(action_table.shape, BF16),
            pltpu.VMEM((1, width), F32),
            pltpu.VMEM((8, LANES), F32),
            pltpu.VMEM((1, width), F32),
            pltpu.VMEM((8, LANES), F32),
            pltpu.VMEM((ITEM_COMPS, items), F32),
            pltpu.VMEM(gate_first.shape, BF16),
            pltpu.VMEM(gate_first.shape, BF16),
            pltpu.VMEM((users, items), F32),
            pltpu.VMEM(item_codes.shape, jnp.int32),
            pltpu.VMEM((width, width), BF16),
            pltpu.VMEM((4 * width // CHUNK, width, CHUNK), BF16),
            pltpu.VMEM((rows, width), BF16),
            pltpu.VMEM((users, items), F32),
            pltpu.VMEM((rows, width), F32),
            dma((3,)),
            dma((13,)),
            dma((4 * width // CHUNK,)),
            pltpu.VMEM((rows, width), F32),
            pltpu.VMEM((rows + 16, width), BF16),
            pltpu.VMEM((rows, width), F32),
            pltpu.VMEM((HEADS, 2, rows, LANES), BF16),
            pltpu.VMEM((HEADS, rows, LANES), BF16),
            pltpu.VMEM((n_events, 2, rows, LANES), BF16),
            pltpu.VMEM((chips, rows, LANES), BF16),
            pltpu.VMEM((chips, rows, LANES), F32),
            pltpu.VMEM((HEADS, rows, LANES), F32),
            pltpu.VMEM(small, F32),
            pltpu.VMEM((n_events - 1,) + small, F32),
            pltpu.VMEM(small, F32),
            pltpu.VMEM((n_events - 1,) + small, F32),
            pltpu.VMEM(small, F32),
            pltpu.VMEM((n_items,) + small, F32),
            pltpu.VMEM((n_items,) + small, F32),
            pltpu.VMEM((n_items - 1,) + small, F32),
            pltpu.VMEM(small, F32),
            pltpu.VMEM((n_events - 1,) + small, F32),
            pltpu.VMEM((COMPS * ITEM_COMPS, users * LANES), F32),
            pltpu.VMEM((ITEM_COMPS, users * 8, LANES), F32),
            pltpu.VMEM((ITEM_COMPS, LANES, items), BF16),
            dma((5,)),
            dma((5,)),
            dma(()),
            dma(()),
            dma((chips,)),
            dma(()),
            dma(()),
            dma(()),
            dma(()),
            dma(()),
            dma(()),
        ],
        compiler_params=pltpu.CompilerParams(
            collective_id=0, has_side_effects=True, vmem_limit_bytes=VMEM_LIMIT
        ),
    )(
        lengths,
        history,
        actions,
        action_table,
        input_gain.reshape(1, width),
        input_gain.reshape(8, LANES),
        output_gain.reshape(1, width),
        output_gain.reshape(8, LANES),
        item_scale.T,
        gate_first,
        gate_second.T,
        teacher,
        item_codes,
        output_weight,
        input_weight,
    )
    return pl.pallas_call(
        write_out,
        out_shape=(
            jax.ShapeDtypeStruct((1, rows, width), BF16),
            jax.ShapeDtypeStruct((users, items), F32),
            jax.ShapeDtypeStruct((1, rows, width), F32),
        ),
        in_specs=[pl.BlockSpec(memory_space=pl.ANY)] * 3,
        out_specs=(hbm, hbm, hbm),
        scratch_shapes=[
            pltpu.VMEM((1, rows, width), BF16),
            pltpu.VMEM((users, items), F32),
            pltpu.VMEM((1, rows, width), F32),
            dma((2, 3)),
        ],
        compiler_params=pltpu.CompilerParams(vmem_limit_bytes=VMEM_LIMIT),
    )(layer, scores, dvalues)


def write_out(layer_in, scores_in, dval_in, layer_out, scores_out, dval_out, layer, scores, dval, sem):
    trips = ((dval_in, dval, dval_out), (layer_in, layer, layer_out), (scores_in, scores, scores_out))
    reads = [pltpu.make_async_copy(a, b, sem.at[0, k]) for k, (a, b, _) in enumerate(trips)]
    writes = [pltpu.make_async_copy(b, c, sem.at[1, k]) for k, (_, b, c) in enumerate(trips)]
    for copy in reads:
        copy.start()
    for first, second in zip(reads, writes):
        first.wait()
        second.start()
    for copy in writes:
        copy.wait()


def solution(mesh):
    in_specs = (
        P("items", "events", None),
        P("items", "events"),
        P(),
        P("items"),
        P(),
        P(),
        P(),
        P(),
        P(("items", "events"), None),
        P(("items", "events"), None),
        P(),
        P(),
        P(None, ("items", "events")),
    )
    out_specs = (
        P("items", "events", None),
        P(None, ("items", "events")),
        P("items", "events", None),
    )
    body = functools.partial(local, mesh.shape["items"], mesh.shape["events"])
    return jax.shard_map(body, mesh=mesh, in_specs=in_specs, out_specs=out_specs, check_vma=False)
```

```python
import functools

import jax
import jax.numpy as jnp
from jax import lax
from jax.experimental import pallas as pl
from jax.experimental.pallas import tpu as pltpu
from jax.sharding import PartitionSpec as P

MESH = pl.DeviceIdType.MESH
HEADS = 8
COMPS = 8
ITEM_COMPS = 8
LENGTH = 2048
LANES = 128
EPS = 1e-05
F32, BF16 = jnp.float32, jnp.bfloat16
CHUNK = 512
VMEM_LIMIT = 64 * 1000 * 1000
ORDER = (4, 6, 5, 7, 2, 3, 0, 1)


def dot(a, b, ca=1, cb=0):
    return lax.dot_general(a, b, (((ca,), (cb,)), ((), ())), preferred_element_type=F32)


def silu(v):
    half = 0.5 * v
    return half * jnp.tanh(half) + half


def sigmoid(v):
    return 0.5 * jnp.tanh(0.5 * v) + 0.5


def iota(shape, dim):
    return lax.broadcasted_iota(jnp.int32, shape, dim)


def cols(h):
    return slice(h * LANES, (h + 1) * LANES)


def mean_all(v, count):
    return jnp.sum(jnp.sum(v, axis=1, keepdims=True), axis=0, keepdims=True) * (1.0 / count)


def to_rows(c):
    return jnp.concatenate([jnp.broadcast_to(c[h : h + 1, :], (8, LANES)) for h in range(8)], axis=1)


def to_compact(rows):
    sub = iota((8, LANES), 0)
    out = jnp.zeros((8, LANES), F32)
    for h in range(8):
        out = out + jnp.where(sub == h, rows[:, cols(h)], 0.0)
    return out


def kernel(
    n_items,
    n_events,
    lengths_ref,
    hist_in,
    actions_in,
    table_in,
    igain_in,
    igain_c_in,
    ogain_in,
    ogain_c_in,
    scale_in,
    g1_in,
    g2t_in,
    teacher_in,
    codes_in,
    wo_in,
    w_in,
    layer_out,
    scores_out,
    dval_out,
    hist,
    actions_ref,
    table,
    igain_ref,
    igain_c_ref,
    ogain_ref,
    ogain_c_ref,
    scale_ref,
    g1_ref,
    g2t_ref,
    teacher_ref,
    codes,
    wo,
    w,
    layer_ref,
    scores_ref,
    dval_ref,
    out_sem,
    in_sem,
    w_sem,
    summed,
    lhs,
    gate_u,
    kv_send,
    q_send,
    kv_all,
    q_all,
    mret,
    mixbuf,
    last_src,
    last_buf,
    part_src,
    part_buf,
    user_src,
    user_buf,
    de_src,
    rs_buf,
    ar_src,
    ar_buf,
    lref,
    dref,
    items_t,
    small_send,
    small_recv,
    loc_sem,
    kv_ssem,
    kv_rsem,
    q_ssem,
    q_rsem,
    fwd_ssem,
    fwd_rsem,
    ret_ssem,
    ret_rsem,
):
    i = lax.axis_index("items")
    e = lax.axis_index("events")
    chips = n_events // 2
    my_chip, core = e // 2, e % 2
    sibling = 2 * my_chip + (1 - core)
    rows = hist.shape[0]
    width = hist.shape[1]
    length = lengths_ref[0]

    pairs = (
        (hist_in.at[0], hist),
        (actions_in, actions_ref),
        (table_in, table),
        (igain_in, igain_ref),
        (igain_c_in, igain_c_ref),
        (ogain_in, ogain_ref),
        (ogain_c_in, ogain_c_ref),
        (scale_in, scale_ref),
        (g1_in, g1_ref),
        (g2t_in, g2t_ref),
        (teacher_in, teacher_ref),
        (codes_in, codes),
        (wo_in, wo),
    )
    loads = [pltpu.make_async_copy(a, b, in_sem.at[k]) for k, (a, b) in enumerate(pairs)]
    wloads = {
        c: pltpu.make_async_copy(
            w_in.at[:, pl.ds(c * CHUNK, CHUNK)], w.at[c], w_sem.at[c]
        )
        for c in ORDER
    }
    for k in range(12):
        loads[k].start()
    for c in ORDER:
        wloads[c].start()
    loads[12].start()

    barrier = pltpu.get_barrier_semaphore()

    def greet_events(k, _):
        pl.semaphore_signal(
            barrier, inc=1, device_id=(i, lax.rem(e + k, n_events)), device_id_type=MESH
        )
        return 0

    def greet_items(k, _):
        pl.semaphore_signal(
            barrier, inc=1, device_id=(lax.rem(i + k, n_items), e), device_id_type=MESH
        )
        return 0

    lax.fori_loop(1, n_events, greet_events, 0)
    lax.fori_loop(1, n_items, greet_items, 0)

    def to_events(src, buf, phase):
        def go(k, _):
            pltpu.make_async_remote_copy(
                src_ref=src,
                dst_ref=buf.at[k - 1],
                send_sem=small_send.at[phase],
                recv_sem=small_recv.at[phase],
                device_id=(i, lax.rem(e + k, n_events)),
                device_id_type=MESH,
            ).start()
            return 0

        lax.fori_loop(1, n_events, go, 0)

    def small_wait(buf, count, sem):
        part = buf.at[pl.ds(0, count)]
        pltpu.make_async_copy(part, part, sem).wait()

    for k in range(5):
        loads[k].wait()
    onehot_t = (iota((16, rows), 0) == jnp.broadcast_to(actions_ref[...], (16, rows))).astype(BF16)
    s_val = hist[...].astype(F32) + dot(onehot_t, table[...], 0, 0)
    summed[...] = s_val
    at_last = (iota((rows, LANES), 0) + e * rows) == (length - 1)
    picked = jnp.concatenate(
        [jnp.sum(jnp.where(at_last, s_val[:, cols(h)], 0.0), axis=0, keepdims=True) for h in range(8)],
        axis=0,
    )
    last_src[...] = picked
    center = s_val - jnp.mean(s_val, axis=1, keepdims=True)
    spread = lax.rsqrt(jnp.mean(center * center, axis=1, keepdims=True) + EPS)
    lhs[pl.ds(0, rows), :] = (center * spread * igain_ref[...]).astype(BF16)

    pl.semaphore_wait(barrier, n_events - 1 + n_items - 1)
    to_events(last_src, last_buf, 0)

    for k in range(5, 12):
        loads[k].wait()
    p_i, q_i = iota((512, 512), 0), iota((512, 512), 1)
    expand = jnp.where(p_i == 4 * (q_i & 127) + (q_i >> 7), 1.0, 0.0).astype(BF16)
    for half in range(2):
        words = codes[:, cols(half)]
        nibbles = jnp.concatenate(
            [(((words >> (4 * n)) & 15).astype(F32) - 7.5).astype(BF16) for n in range(4)], axis=1
        )
        raw = dot(expand, nibbles, 1, 1)
        for j in range(4):
            c = half * 4 + j
            items_t[c] = (raw[j * LANES : (j + 1) * LANES] * scale_ref[c : c + 1, :]).astype(BF16)
    logit_count = COMPS * ITEM_COMPS
    r_i, s_i = iota((logit_count, logit_count), 0), iota((logit_count, logit_count), 1)
    perm = jnp.where(s_i == (r_i & 7) * 8 + (r_i >> 3), 1.0, 0.0).astype(BF16)
    g1, g2t = g1_ref[...], g2t_ref[...]
    m_first_t = dot(g1, perm, 0, 1).astype(BF16)
    m_first = dot(perm, g1).astype(BF16)
    m_second_t = dot(perm, g2t).astype(BF16)
    m_second = dot(g2t, perm, 0, 1).astype(BF16)

    normed = lhs[pl.ds(0, rows), :]
    keep_row = (iota((rows, LANES), 0) + e * rows) < length
    for c in (4, 6, 5, 7):
        wloads[c].wait()
        y = silu(dot(normed, w[c]))
        for j in range(CHUNK // LANES):
            head = (c % 2) * (CHUNK // LANES) + j
            block = y[:, cols(j)]
            if c < 6:
                kv_send[head, 0] = block.astype(BF16)
            else:
                kv_send[head, 1] = jnp.where(keep_row, block, 0.0).astype(BF16)

    small_wait(last_buf, n_events - 1, small_recv.at[0])
    summed_c = last_src[...]
    for k in range(n_events - 1):
        summed_c = summed_c + last_buf[k]
    center = summed_c - mean_all(summed_c, width)
    spread = lax.rsqrt(mean_all(center * center, width) + EPS)
    last_rows = to_rows(center * spread * igain_c_ref[...])
    lhs[pl.ds(rows, 16), :] = jnp.concatenate([last_rows, last_rows], axis=0).astype(BF16)

    both = lhs[...]
    sub = iota((8, LANES), 0)
    q_scores = jnp.zeros((8, rows), F32)
    for c in (2, 3):
        wloads[c].wait()
        y = silu(dot(both, w[c]))
        for j in range(CHUNK // LANES):
            head = (c % 2) * (CHUNK // LANES) + j
            q_send[head] = y[:rows, cols(j)].astype(BF16)
            q_diag = jnp.where(sub == head, y[rows : rows + 8, cols(j)], 0.0).astype(BF16)
            q_scores = q_scores + dot(q_diag, kv_send[head, 0], 1, 1)

    inv = width // HEADS
    keep_col = (iota((8, rows), 1) + e * rows) < length
    w_last = jnp.where(keep_col, silu(q_scores * inv ** (-0.5)) * (1.0 / LENGTH), 0.0).astype(BF16)
    part = jnp.zeros((8, LANES), F32)
    for head in range(HEADS):
        part = part + jnp.where(sub == head, dot(w_last, kv_send[head, 1]), 0.0)
    part_src[...] = part
    to_events(part_src, part_buf, 1)

    gate_rows = []
    for c in (0, 1):
        wloads[c].wait()
        y = silu(dot(both, w[c]))
        gate_u[:, c * CHUNK : (c + 1) * CHUNK] = y[:rows]
        gate_rows.append(y[rows : rows + 8])
    gate_c = to_compact(jnp.concatenate(gate_rows, axis=1))

    small_wait(part_buf, n_events - 1, small_recv.at[1])
    mixed_c = part_src[...]
    for k in range(n_events - 1):
        mixed_c = mixed_c + part_buf[k]
    center_c = mixed_c - mean_all(mixed_c, width)
    spread_c = lax.rsqrt(mean_all(center_c * center_c, width) + EPS)
    normal_c = center_c * spread_c
    gated_c = normal_c * ogain_c_ref[...] * gate_c
    loads[12].wait()
    user_rows = dot(to_rows(gated_c).astype(BF16), wo[...])
    user_c = (summed_c + to_compact(user_rows)).astype(BF16).astype(F32)
    user_src[...] = user_c
    user_buf[i] = user_c

    def send_user(k, _):
        pltpu.make_async_remote_copy(
            src_ref=user_src,
            dst_ref=user_buf.at[i],
            send_sem=small_send.at[2],
            recv_sem=small_recv.at[2],
            device_id=(lax.rem(i + k, n_items), e),
            device_id_type=MESH,
        ).start()
        return 0

    lax.fori_loop(1, n_items, send_user, 0)

    owner = lax.rem(e + my_chip, 2)

    def kv_copy(k, target_core, block, sem_s, sem_r):
        chip = lax.rem(my_chip + k, chips)
        return pltpu.make_async_remote_copy(
            src_ref=kv_send.at[chip],
            dst_ref=kv_all.at[block],
            send_sem=sem_s,
            recv_sem=sem_r,
            device_id=(i, 2 * chip + target_core),
            device_id_type=MESH,
        )

    own_kv = pltpu.make_async_copy(kv_send.at[my_chip], kv_all.at[e], loc_sem)
    own_kv.start()
    sib_kv = pltpu.make_async_remote_copy(
        src_ref=kv_send.at[my_chip],
        dst_ref=kv_all.at[e],
        send_sem=fwd_ssem,
        recv_sem=fwd_rsem,
        device_id=(i, sibling),
        device_id_type=MESH,
    )
    sib_kv.start()

    def send_kv(k, _):
        kv_copy(k, core, e, kv_ssem, kv_rsem.at[k]).start()
        return 0

    lax.fori_loop(1, chips, send_kv, 0)

    def q_remote(chip):
        return pltpu.make_async_remote_copy(
            src_ref=q_send.at[chip],
            dst_ref=q_all.at[my_chip],
            send_sem=q_ssem,
            recv_sem=q_rsem,
            device_id=(i, 2 * chip + owner),
            device_id_type=MESH,
        )

    def send_q(k, _):
        q_remote(lax.rem(my_chip + k, chips)).start()
        return 0

    lax.fori_loop(1, chips, send_q, 0)

    @pl.when(owner == core)
    def _():
        pltpu.make_async_copy(q_send.at[my_chip], q_all.at[my_chip], q_rsem).start()

    @pl.when(owner != core)
    def _():
        q_remote(my_chip).start()

    users = n_items
    small_wait(user_buf, n_items - 1, small_recv.at[2])
    everyone = user_buf[...].reshape(users * 8, LANES).astype(BF16)
    for c in range(ITEM_COMPS):
        part_l = dot(everyone, items_t[c])
        for b in range(users):
            lref[c * 8 : (c + 1) * 8, cols(b)] = part_l[b * 8 : (b + 1) * 8]
    for b0 in range(0, users, 2):
        span = slice(b0 * LANES, (b0 + 2) * LANES)
        logits = lref[:, span]
        pre = dot(m_first_t, logits.astype(BF16))
        sig = sigmoid(pre)
        gates = sigmoid(dot(m_second_t, (pre * sig).astype(BF16)))
        gl = gates * logits
        score = jnp.sum(gl, axis=0, keepdims=True)
        targets = jnp.concatenate(
            [teacher_ref[b0 : b0 + 1, :], teacher_ref[b0 + 1 : b0 + 2, :]], axis=1
        )
        scores_ref[b0 : b0 + 1, :] = score[:, :LANES]
        scores_ref[b0 + 1 : b0 + 2, :] = score[:, LANES:]
        slope = (gl * (1.0 - gates)).astype(BF16)
        back = dot(m_second, slope) * (sig * (1.0 + pre * (1.0 - sig)))
        dlog = (score - targets) * (gates + dot(m_first, back.astype(BF16)))
        for c in range(ITEM_COMPS):
            for j in range(2):
                b = b0 + j
                dref[c, b * 8 : (b + 1) * 8, :] = dlog[c * 8 : (c + 1) * 8, cols(j)]
    demb = jnp.zeros((users * 8, LANES), F32)
    for c in range(ITEM_COMPS):
        demb = demb + dot(dref[c].astype(BF16), items_t[c], 1, 1)
    de_src[...] = demb.reshape(users, 8, LANES)

    def send_de(k, _):
        other = lax.rem(i + k, n_items)
        pltpu.make_async_remote_copy(
            src_ref=de_src.at[other],
            dst_ref=rs_buf.at[k - 1],
            send_sem=small_send.at[3],
            recv_sem=small_recv.at[3],
            device_id=(other, e),
            device_id_type=MESH,
        ).start()
        return 0

    lax.fori_loop(1, n_items, send_de, 0)

    out_scores = pltpu.make_async_copy(scores_ref, scores_out, out_sem.at[1])
    out_scores.start()

    own_kv.wait()

    def forward(k, _):
        source = 2 * lax.rem(my_chip + chips - k, chips) + core
        pltpu.make_async_copy(kv_all.at[source], kv_all.at[source], kv_rsem.at[k]).wait()
        pltpu.make_async_remote_copy(
            src_ref=kv_all.at[source],
            dst_ref=kv_all.at[source],
            send_sem=fwd_ssem,
            recv_sem=fwd_rsem,
            device_id=(i, sibling),
            device_id_type=MESH,
        ).start()
        return 0

    lax.fori_loop(1, chips, forward, 0)

    small_wait(rs_buf, n_items - 1, small_recv.at[3])
    red = de_src[i]
    for k in range(n_items - 1):
        red = red + rs_buf[k]
    ar_src[...] = red
    to_events(ar_src, ar_buf, 4)

    half_blocks = kv_all.at[pl.ds(0, chips)]
    pltpu.make_async_copy(half_blocks, half_blocks, fwd_rsem).wait()
    pltpu.make_async_copy(q_all, q_all, q_rsem).wait()
    half_scale = 0.5 * inv ** (-0.5)
    for n in range(chips):
        query = q_all[n]
        odd = lax.rem(core + n, 2)
        acc = jnp.zeros((rows, LANES), F32)
        for m in range(n + 1):
            key = jnp.concatenate([kv_all[2 * m, 0], kv_all[2 * m + 1, 0]], axis=0)
            value = jnp.concatenate([kv_all[2 * m, 1], kv_all[2 * m + 1, 1]], axis=0)
            half = dot(query, key, 1, 1) * half_scale
            weight = half * jnp.tanh(half) + half
            if m == n:
                causal = iota((rows, 2 * rows), 1) <= iota((rows, 2 * rows), 0) + odd * rows
                weight = jnp.where(causal, weight, 0.0)
            acc = acc + dot(weight.astype(BF16), value)
        mret[n] = acc.astype(BF16)

    def ret_remote(n, target):
        return pltpu.make_async_remote_copy(
            src_ref=mret.at[n],
            dst_ref=mixbuf.at[my_chip],
            send_sem=ret_ssem,
            recv_sem=ret_rsem,
            device_id=(i, target),
            device_id_type=MESH,
        )

    def ret_target(n):
        return 2 * n + lax.rem(n + core, 2)

    def send_ret(n, _):
        target = ret_target(n)

        @pl.when(target == e)
        def _():
            pltpu.make_async_copy(mret.at[n], mixbuf.at[my_chip], ret_rsem).start()

        @pl.when(target != e)
        def _():
            ret_remote(n, target).start()

        return 0

    lax.fori_loop(0, chips, send_ret, 0)

    small_wait(ar_buf, n_events - 1, small_recv.at[4])
    total = ar_src[...]
    for k in range(n_events - 1):
        total = total + ar_buf[k]
    dgated = to_compact(dot(to_rows(total).astype(BF16), wo[...], 1, 1))
    s_c = dgated * gate_c * ogain_c_ref[...]
    dmixed = (
        s_c - mean_all(s_c, width) - normal_c * mean_all(s_c * normal_c, width)
    ) * spread_c
    diag = jnp.concatenate([jnp.where(sub == h, dmixed, 0.0) for h in range(8)], axis=1)
    hi = diag.astype(BF16)
    lo = (diag - hi.astype(F32)).astype(BF16)
    w2 = jnp.concatenate([w_last.astype(F32), w_last.astype(F32)], axis=0).astype(BF16)
    hilo = jnp.concatenate([hi.astype(F32), lo.astype(F32)], axis=0).astype(BF16)
    dval_ref[...] = dot(w2, hilo, 0, 0)

    out_dval = pltpu.make_async_copy(dval_ref, dval_out.at[0], out_sem.at[2])
    out_dval.start()

    pltpu.make_async_copy(mixbuf, mixbuf, ret_rsem).wait()
    scale = 1.0 / LENGTH
    tot = jnp.zeros((rows, 1), F32)
    for h in range(HEADS):
        tot = tot + jnp.sum(mixbuf[h].astype(F32), axis=1, keepdims=True)
    mean = tot * (1.0 / width)
    var = jnp.zeros((rows, 1), F32)
    for h in range(HEADS):
        c_h = (mixbuf[h].astype(F32) - mean) * scale
        var = var + jnp.sum(c_h * c_h, axis=1, keepdims=True)
    spread = lax.rsqrt(var * (1.0 / width) + EPS) * scale
    gated = jnp.concatenate(
        [
            ((mixbuf[h].astype(F32) - mean) * spread * ogain_ref[:, cols(h)] * gate_u[:, cols(h)]).astype(BF16)
            for h in range(HEADS)
        ],
        axis=1,
    )
    layer_ref[...] = (summed[...] + dot(gated, wo[...])).astype(BF16)

    out_layer = pltpu.make_async_copy(layer_ref, layer_out.at[0], out_sem.at[0])
    out_layer.start()

    small_wait(last_buf, n_events - 1, small_send.at[0])
    small_wait(part_buf, n_events - 1, small_send.at[1])
    small_wait(user_buf, n_items - 1, small_send.at[2])
    small_wait(rs_buf, n_items - 1, small_send.at[3])
    small_wait(ar_buf, n_events - 1, small_send.at[4])
    kv_part = kv_send.at[pl.ds(0, chips - 1)]
    pltpu.make_async_copy(kv_part, kv_part, kv_ssem).wait()
    pltpu.make_async_copy(kv_send, kv_send, fwd_ssem).wait()
    q_part = q_send.at[pl.ds(0, chips - 1)]
    pltpu.make_async_copy(q_part, q_part, q_ssem).wait()

    @pl.when(owner != core)
    def _():
        q_remote(my_chip).wait_send()

    def ret_wait(n, _):
        target = ret_target(n)

        @pl.when(target != e)
        def _():
            ret_remote(n, target).wait_send()

        return 0

    lax.fori_loop(0, chips, ret_wait, 0)
    out_scores.wait()
    out_dval.wait()
    out_layer.wait()


def local(
    n_items,
    n_events,
    history,
    actions,
    action_table,
    lengths,
    input_gain,
    input_weight,
    output_gain,
    output_weight,
    item_codes,
    item_scale,
    gate_first,
    gate_second,
    teacher,
):
    _, rows, width = history.shape
    chips = n_events // 2
    items = item_codes.shape[0]
    users = n_items
    small = (8, LANES)
    smem = pl.BlockSpec(memory_space=pltpu.SMEM)
    hbm = pl.BlockSpec(memory_space=pl.ANY)
    dma = pltpu.SemaphoreType.DMA
    layer, scores, dvalues = pl.pallas_call(
        functools.partial(kernel, n_items, n_events),
        out_shape=(
            jax.ShapeDtypeStruct((1, rows, width), BF16),
            jax.ShapeDtypeStruct((users, items), F32),
            jax.ShapeDtypeStruct((1, rows, width), F32),
        ),
        in_specs=[smem] + [hbm] * 14,
        out_specs=(hbm, hbm, hbm),
        scratch_shapes=[
            pltpu.VMEM((rows, width), BF16),
            pltpu.VMEM(actions.shape, jnp.int32),
            pltpu.VMEM(action_table.shape, BF16),
            pltpu.VMEM((1, width), F32),
            pltpu.VMEM((8, LANES), F32),
            pltpu.VMEM((1, width), F32),
            pltpu.VMEM((8, LANES), F32),
            pltpu.VMEM((ITEM_COMPS, items), F32),
            pltpu.VMEM(gate_first.shape, BF16),
            pltpu.VMEM(gate_first.shape, BF16),
            pltpu.VMEM((users, items), F32),
            pltpu.VMEM(item_codes.shape, jnp.int32),
            pltpu.VMEM((width, width), BF16),
            pltpu.VMEM((4 * width // CHUNK, width, CHUNK), BF16),
            pltpu.VMEM((rows, width), BF16),
            pltpu.VMEM((users, items), F32),
            pltpu.VMEM((rows, width), F32),
            dma((3,)),
            dma((13,)),
            dma((4 * width // CHUNK,)),
            pltpu.VMEM((rows, width), F32),
            pltpu.VMEM((rows + 16, width), BF16),
            pltpu.VMEM((rows, width), F32),
            pltpu.VMEM((HEADS, 2, rows, LANES), BF16),
            pltpu.VMEM((HEADS, rows, LANES), BF16),
            pltpu.VMEM((n_events, 2, rows, LANES), BF16),
            pltpu.VMEM((chips, rows, LANES), BF16),
            pltpu.VMEM((chips, rows, LANES), BF16),
            pltpu.VMEM((HEADS, rows, LANES), BF16),
            pltpu.VMEM(small, F32),
            pltpu.VMEM((n_events - 1,) + small, F32),
            pltpu.VMEM(small, F32),
            pltpu.VMEM((n_events - 1,) + small, F32),
            pltpu.VMEM(small, F32),
            pltpu.VMEM((n_items,) + small, F32),
            pltpu.VMEM((n_items,) + small, F32),
            pltpu.VMEM((n_items - 1,) + small, F32),
            pltpu.VMEM(small, F32),
            pltpu.VMEM((n_events - 1,) + small, F32),
            pltpu.VMEM((COMPS * ITEM_COMPS, users * LANES), F32),
            pltpu.VMEM((ITEM_COMPS, users * 8, LANES), F32),
            pltpu.VMEM((ITEM_COMPS, LANES, items), BF16),
            dma((5,)),
            dma((5,)),
            dma(()),
            dma(()),
            dma((chips,)),
            dma(()),
            dma(()),
            dma(()),
            dma(()),
            dma(()),
            dma(()),
        ],
        compiler_params=pltpu.CompilerParams(
            collective_id=0, has_side_effects=True, vmem_limit_bytes=VMEM_LIMIT
        ),
    )(
        lengths,
        history,
        actions,
        action_table,
        input_gain.reshape(1, width),
        input_gain.reshape(8, LANES),
        output_gain.reshape(1, width),
        output_gain.reshape(8, LANES),
        item_scale.T,
        gate_first,
        gate_second.T,
        teacher,
        item_codes,
        output_weight,
        input_weight,
    )
    return pl.pallas_call(
        write_out,
        out_shape=(
            jax.ShapeDtypeStruct((1, rows, width), BF16),
            jax.ShapeDtypeStruct((users, items), F32),
            jax.ShapeDtypeStruct((1, rows, width), F32),
        ),
        in_specs=[pl.BlockSpec(memory_space=pl.ANY)] * 3,
        out_specs=(hbm, hbm, hbm),
        scratch_shapes=[
            pltpu.VMEM((1, rows, width), BF16),
            pltpu.VMEM((users, items), F32),
            pltpu.VMEM((1, rows, width), F32),
            dma((2, 3)),
        ],
        compiler_params=pltpu.CompilerParams(vmem_limit_bytes=VMEM_LIMIT),
    )(layer, scores, dvalues)


def write_out(layer_in, scores_in, dval_in, layer_out, scores_out, dval_out, layer, scores, dval, sem):
    trips = ((dval_in, dval, dval_out), (layer_in, layer, layer_out), (scores_in, scores, scores_out))
    reads = [pltpu.make_async_copy(a, b, sem.at[0, k]) for k, (a, b, _) in enumerate(trips)]
    writes = [pltpu.make_async_copy(b, c, sem.at[1, k]) for k, (_, b, c) in enumerate(trips)]
    for copy in reads:
        copy.start()
    for first, second in zip(reads, writes):
        first.wait()
        second.start()
    for copy in writes:
        copy.wait()


def solution(mesh):
    in_specs = (
        P("items", "events", None),
        P("items", "events"),
        P(),
        P("items"),
        P(),
        P(),
        P(),
        P(),
        P(("items", "events"), None),
        P(("items", "events"), None),
        P(),
        P(),
        P(None, ("items", "events")),
    )
    out_specs = (
        P("items", "events", None),
        P(None, ("items", "events")),
        P("items", "events", None),
    )
    body = functools.partial(local, mesh.shape["items"], mesh.shape["events"])
    return jax.shard_map(body, mesh=mesh, in_specs=in_specs, out_specs=out_specs, check_vma=False)
```

```python
import functools

import jax
import jax.numpy as jnp
from jax import lax
from jax.experimental import pallas as pl
from jax.experimental.pallas import tpu as pltpu
from jax.sharding import PartitionSpec as P

MESH = pl.DeviceIdType.MESH
HEADS = 8
COMPS = 8
ITEM_COMPS = 8
LENGTH = 2048
LANES = 128
EPS = 1e-05
F32, BF16 = jnp.float32, jnp.bfloat16
CHUNK = 512
GROUP = 16
VMEM_LIMIT = 64 * 1000 * 1000
ORDER = (4, 6, 5, 7, 2, 3, 0, 1)


def dot(a, b, ca=1, cb=0):
    return lax.dot_general(a, b, (((ca,), (cb,)), ((), ())), preferred_element_type=F32)


def silu(v):
    half = 0.5 * v
    return half * jnp.tanh(half) + half


def sigmoid(v):
    return 0.5 * jnp.tanh(0.5 * v) + 0.5


def iota(shape, dim):
    return lax.broadcasted_iota(jnp.int32, shape, dim)


def cols(h):
    return slice(h * LANES, (h + 1) * LANES)


def mean_all(v, count):
    return jnp.sum(jnp.sum(v, axis=1, keepdims=True), axis=0, keepdims=True) * (1.0 / count)


def to_rows(c):
    return jnp.concatenate([jnp.broadcast_to(c[h : h + 1, :], (8, LANES)) for h in range(8)], axis=1)


def to_compact(rows):
    sub = iota((8, LANES), 0)
    out = jnp.zeros((8, LANES), F32)
    for h in range(8):
        out = out + jnp.where(sub == h, rows[:, cols(h)], 0.0)
    return out


def kernel(
    n_items,
    n_events,
    lengths_ref,
    hist_in,
    actions_in,
    table_in,
    igain_in,
    igain_c_in,
    ogain_in,
    ogain_c_in,
    scale_in,
    g1_in,
    g2t_in,
    teacher_in,
    codes_in,
    wo_in,
    w_in,
    layer_out,
    scores_out,
    dval_out,
    hist,
    actions_ref,
    table,
    igain_ref,
    igain_c_ref,
    ogain_ref,
    ogain_c_ref,
    scale_ref,
    g1_ref,
    g2t_ref,
    teacher_ref,
    codes,
    wo,
    w,
    layer_ref,
    scores_ref,
    dval_ref,
    out_sem,
    in_sem,
    w_sem,
    summed,
    lhs,
    gate_u,
    kv_send,
    q_send,
    kv_all,
    q_all,
    mret,
    mixbuf,
    last_src,
    last_buf,
    part_src,
    part_buf,
    user_src,
    user_buf,
    de_src,
    rs_buf,
    ar_src,
    ar_buf,
    lref,
    dref,
    items_t,
    items_n,
    small_send,
    small_recv,
    loc_sem,
    kv_ssem,
    kv_rsem,
    q_ssem,
    q_rsem,
    fwd_ssem,
    fwd_rsem,
    ret_ssem,
    ret_rsem,
):
    i = lax.axis_index("items")
    e = lax.axis_index("events")
    chips = n_events // 2
    my_chip, core = e // 2, e % 2
    sibling = 2 * my_chip + (1 - core)
    rows = hist.shape[0]
    width = hist.shape[1]
    length = lengths_ref[0]

    pairs = (
        (hist_in.at[0], hist),
        (actions_in, actions_ref),
        (table_in, table),
        (igain_in, igain_ref),
        (igain_c_in, igain_c_ref),
        (ogain_in, ogain_ref),
        (ogain_c_in, ogain_c_ref),
        (scale_in, scale_ref),
        (g1_in, g1_ref),
        (g2t_in, g2t_ref),
        (teacher_in, teacher_ref),
        (codes_in, codes),
        (wo_in, wo),
    )
    loads = [pltpu.make_async_copy(a, b, in_sem.at[k]) for k, (a, b) in enumerate(pairs)]
    wloads = {
        c: pltpu.make_async_copy(
            w_in.at[:, pl.ds(c * CHUNK, CHUNK)], w.at[c], w_sem.at[c]
        )
        for c in ORDER
    }
    for k in range(12):
        loads[k].start()
    for c in ORDER:
        wloads[c].start()
    loads[12].start()

    barrier = pltpu.get_barrier_semaphore()

    def greet_events(k, _):
        pl.semaphore_signal(
            barrier, inc=1, device_id=(i, lax.rem(e + k, n_events)), device_id_type=MESH
        )
        return 0

    def greet_items(k, _):
        pl.semaphore_signal(
            barrier, inc=1, device_id=(lax.rem(i + k, n_items), e), device_id_type=MESH
        )
        return 0

    lax.fori_loop(1, n_events, greet_events, 0)
    lax.fori_loop(1, n_items, greet_items, 0)

    def to_events(src, buf, phase):
        def go(k, _):
            pltpu.make_async_remote_copy(
                src_ref=src,
                dst_ref=buf.at[k - 1],
                send_sem=small_send.at[phase],
                recv_sem=small_recv.at[phase],
                device_id=(i, lax.rem(e + k, n_events)),
                device_id_type=MESH,
            ).start()
            return 0

        lax.fori_loop(1, n_events, go, 0)

    def small_wait(buf, count, sem):
        part = buf.at[pl.ds(0, count)]
        pltpu.make_async_copy(part, part, sem).wait()

    for k in range(5):
        loads[k].wait()
    onehot_t = (iota((16, rows), 0) == jnp.broadcast_to(actions_ref[...], (16, rows))).astype(BF16)
    s_val = hist[...].astype(F32) + dot(onehot_t, table[...], 0, 0)
    summed[...] = s_val
    at_last = (iota((rows, LANES), 0) + e * rows) == (length - 1)
    picked = jnp.concatenate(
        [jnp.sum(jnp.where(at_last, s_val[:, cols(h)], 0.0), axis=0, keepdims=True) for h in range(8)],
        axis=0,
    )
    last_src[...] = picked
    center = s_val - jnp.mean(s_val, axis=1, keepdims=True)
    spread = lax.rsqrt(jnp.mean(center * center, axis=1, keepdims=True) + EPS)
    lhs[pl.ds(0, rows), :] = (center * spread * igain_ref[...]).astype(BF16)

    pl.semaphore_wait(barrier, n_events - 1 + n_items - 1)
    to_events(last_src, last_buf, 0)

    for k in range(5, 12):
        loads[k].wait()
    p_i, q_i = iota((512, 512), 0), iota((512, 512), 1)
    expand = jnp.where(p_i == 4 * (q_i & 127) + (q_i >> 7), 1.0, 0.0).astype(BF16)
    for half in range(2):
        words = codes[:, cols(half)]
        nibbles = jnp.concatenate(
            [(((words >> (4 * n)) & 15).astype(F32) - 7.5).astype(BF16) for n in range(4)], axis=1
        )
        raw = dot(expand, nibbles, 1, 1)
        for j in range(4):
            c = half * 4 + j
            vector = raw[j * LANES : (j + 1) * LANES] * scale_ref[c : c + 1, :]
            items_t[:, cols(c)] = vector.astype(BF16)
            items_n[c * LANES : (c + 1) * LANES, :] = vector.T.astype(BF16)
    logit_count = COMPS * ITEM_COMPS
    r_i, s_i = iota((logit_count, logit_count), 0), iota((logit_count, logit_count), 1)
    perm = jnp.where(s_i == (r_i & 7) * 8 + (r_i >> 3), 1.0, 0.0).astype(BF16)
    g1, g2t = g1_ref[...], g2t_ref[...]
    m_first_t = dot(g1, perm, 0, 1).astype(BF16)
    m_first = dot(perm, g1).astype(BF16)
    m_second_t = dot(perm, g2t).astype(BF16)
    m_second = dot(g2t, perm, 0, 1).astype(BF16)

    normed = lhs[pl.ds(0, rows), :]
    keep_row = (iota((rows, LANES), 0) + e * rows) < length
    for c in (4, 6, 5, 7):
        wloads[c].wait()
        y = silu(dot(normed, w[c]))
        for j in range(CHUNK // LANES):
            head = (c % 2) * (CHUNK // LANES) + j
            block = y[:, cols(j)]
            if c < 6:
                kv_send[head, 0] = block.astype(BF16)
            else:
                kv_send[head, 1] = jnp.where(keep_row, block, 0.0).astype(BF16)

    owner = lax.rem(e + my_chip, 2)

    def kv_copy(k, target_core, block, sem_s, sem_r):
        chip = lax.rem(my_chip + k, chips)
        return pltpu.make_async_remote_copy(
            src_ref=kv_send.at[chip],
            dst_ref=kv_all.at[block],
            send_sem=sem_s,
            recv_sem=sem_r,
            device_id=(i, 2 * chip + target_core),
            device_id_type=MESH,
        )

    own_kv = pltpu.make_async_copy(kv_send.at[my_chip], kv_all.at[e], loc_sem)
    own_kv.start()
    sib_kv = pltpu.make_async_remote_copy(
        src_ref=kv_send.at[my_chip],
        dst_ref=kv_all.at[e],
        send_sem=fwd_ssem,
        recv_sem=fwd_rsem,
        device_id=(i, sibling),
        device_id_type=MESH,
    )
    sib_kv.start()

    def send_kv(k, _):
        kv_copy(k, core, e, kv_ssem, kv_rsem.at[k]).start()
        return 0

    lax.fori_loop(1, chips, send_kv, 0)


    small_wait(last_buf, n_events - 1, small_recv.at[0])
    summed_c = last_src[...]
    for k in range(n_events - 1):
        summed_c = summed_c + last_buf[k]
    center = summed_c - mean_all(summed_c, width)
    spread = lax.rsqrt(mean_all(center * center, width) + EPS)
    last_rows = to_rows(center * spread * igain_c_ref[...])
    lhs[pl.ds(rows, 16), :] = jnp.concatenate([last_rows, last_rows], axis=0).astype(BF16)

    both = lhs[...]
    sub = iota((8, LANES), 0)
    q_scores = jnp.zeros((8, rows), F32)
    for c in (2, 3):
        wloads[c].wait()
        y = silu(dot(both, w[c]))
        for j in range(CHUNK // LANES):
            head = (c % 2) * (CHUNK // LANES) + j
            q_send[head] = y[:rows, cols(j)].astype(BF16)
            q_diag = jnp.where(sub == head, y[rows : rows + 8, cols(j)], 0.0).astype(BF16)
            q_scores = q_scores + dot(q_diag, kv_send[head, 0], 1, 1)

    inv = width // HEADS
    keep_col = (iota((8, rows), 1) + e * rows) < length
    w_last = jnp.where(keep_col, silu(q_scores * inv ** (-0.5)) * (1.0 / LENGTH), 0.0).astype(BF16)
    part = jnp.zeros((8, LANES), F32)
    for head in range(HEADS):
        part = part + jnp.where(sub == head, dot(w_last, kv_send[head, 1]), 0.0)
    part_src[...] = part
    to_events(part_src, part_buf, 1)

    gate_rows = []
    for c in (0, 1):
        wloads[c].wait()
        y = silu(dot(both, w[c]))
        gate_u[:, c * CHUNK : (c + 1) * CHUNK] = y[:rows]
        gate_rows.append(y[rows : rows + 8])
    gate_c = to_compact(jnp.concatenate(gate_rows, axis=1))

    small_wait(part_buf, n_events - 1, small_recv.at[1])
    mixed_c = part_src[...]
    for k in range(n_events - 1):
        mixed_c = mixed_c + part_buf[k]
    center_c = mixed_c - mean_all(mixed_c, width)
    spread_c = lax.rsqrt(mean_all(center_c * center_c, width) + EPS)
    normal_c = center_c * spread_c
    gated_c = normal_c * ogain_c_ref[...] * gate_c
    loads[12].wait()
    user_rows = dot(to_rows(gated_c).astype(BF16), wo[...])
    user_c = (summed_c + to_compact(user_rows)).astype(BF16).astype(F32)
    user_src[...] = user_c
    user_buf[i] = user_c

    def send_user(k, _):
        pltpu.make_async_remote_copy(
            src_ref=user_src,
            dst_ref=user_buf.at[i],
            send_sem=small_send.at[2],
            recv_sem=small_recv.at[2],
            device_id=(lax.rem(i + k, n_items), e),
            device_id_type=MESH,
        ).start()
        return 0

    lax.fori_loop(1, n_items, send_user, 0)

    def q_remote(chip):
        return pltpu.make_async_remote_copy(
            src_ref=q_send.at[chip],
            dst_ref=q_all.at[my_chip],
            send_sem=q_ssem,
            recv_sem=q_rsem,
            device_id=(i, 2 * chip + owner),
            device_id_type=MESH,
        )

    def send_q(k, _):
        q_remote(lax.rem(my_chip + k, chips)).start()
        return 0

    lax.fori_loop(1, chips, send_q, 0)

    @pl.when(owner == core)
    def _():
        pltpu.make_async_copy(q_send.at[my_chip], q_all.at[my_chip], q_rsem).start()

    @pl.when(owner != core)
    def _():
        q_remote(my_chip).start()

    own_kv.wait()

    def forward(k, _):
        source = 2 * lax.rem(my_chip + chips - k, chips) + core
        pltpu.make_async_copy(kv_all.at[source], kv_all.at[source], kv_rsem.at[k]).wait()
        pltpu.make_async_remote_copy(
            src_ref=kv_all.at[source],
            dst_ref=kv_all.at[source],
            send_sem=fwd_ssem,
            recv_sem=fwd_rsem,
            device_id=(i, sibling),
            device_id_type=MESH,
        ).start()
        return 0

    lax.fori_loop(1, chips, forward, 0)


    users = n_items
    small_wait(user_buf, n_items - 1, small_recv.at[2])
    everyone = user_buf[...].reshape(users * 8, LANES).astype(BF16)
    part_l = dot(everyone, items_t[...])
    for c in range(ITEM_COMPS):
        for b in range(users):
            lref[c * 8 : (c + 1) * 8, cols(b)] = part_l[b * 8 : (b + 1) * 8, cols(c)]
    for b0 in range(0, users, GROUP):
        logits = lref[:, b0 * LANES : (b0 + GROUP) * LANES]
        pre = dot(m_first_t, logits.astype(BF16))
        sig = sigmoid(pre)
        gates = sigmoid(dot(m_second_t, (pre * sig).astype(BF16)))
        gl = gates * logits
        score = jnp.sum(gl, axis=0, keepdims=True)
        targets = jnp.concatenate([teacher_ref[b0 + j : b0 + j + 1, :] for j in range(GROUP)], axis=1)
        slope = (gl * (1.0 - gates)).astype(BF16)
        back = dot(m_second, slope) * (sig * (1.0 + pre * (1.0 - sig)))
        dlog = (score - targets) * (gates + dot(m_first, back.astype(BF16)))
        for j in range(GROUP):
            b = b0 + j
            scores_ref[b : b + 1, :] = score[:, cols(j)]
            for c in range(ITEM_COMPS):
                dref[b * 8 : (b + 1) * 8, cols(c)] = dlog[c * 8 : (c + 1) * 8, cols(j)]
    demb = dot(dref[...].astype(BF16), items_n[...])
    de_src[...] = demb.reshape(users, 8, LANES)

    def send_de(k, _):
        other = lax.rem(i + k, n_items)
        pltpu.make_async_remote_copy(
            src_ref=de_src.at[other],
            dst_ref=rs_buf.at[k - 1],
            send_sem=small_send.at[3],
            recv_sem=small_recv.at[3],
            device_id=(other, e),
            device_id_type=MESH,
        ).start()
        return 0

    lax.fori_loop(1, n_items, send_de, 0)

    out_scores = pltpu.make_async_copy(scores_ref, scores_out, out_sem.at[1])
    out_scores.start()

    half_blocks = kv_all.at[pl.ds(0, chips)]
    pltpu.make_async_copy(half_blocks, half_blocks, fwd_rsem).wait()
    pltpu.make_async_copy(q_all, q_all, q_rsem).wait()
    half_scale = 0.5 * inv ** (-0.5)
    for n in range(chips):
        query = q_all[n]
        odd = lax.rem(core + n, 2)
        acc = jnp.zeros((rows, LANES), F32)
        for m in range(n + 1):
            key = jnp.concatenate([kv_all[2 * m, 0], kv_all[2 * m + 1, 0]], axis=0)
            value = jnp.concatenate([kv_all[2 * m, 1], kv_all[2 * m + 1, 1]], axis=0)
            half = dot(query, key, 1, 1) * half_scale
            weight = half * jnp.tanh(half) + half
            if m == n:
                causal = iota((rows, 2 * rows), 1) <= iota((rows, 2 * rows), 0) + odd * rows
                weight = jnp.where(causal, weight, 0.0)
            acc = acc + dot(weight.astype(BF16), value)
        mret[n] = acc.astype(BF16)

    def ret_remote(n, target):
        return pltpu.make_async_remote_copy(
            src_ref=mret.at[n],
            dst_ref=mixbuf.at[my_chip],
            send_sem=ret_ssem,
            recv_sem=ret_rsem,
            device_id=(i, target),
            device_id_type=MESH,
        )

    def ret_target(n):
        return 2 * n + lax.rem(n + core, 2)

    def send_ret(n, _):
        target = ret_target(n)

        @pl.when(target == e)
        def _():
            pltpu.make_async_copy(mret.at[n], mixbuf.at[my_chip], ret_rsem).start()

        @pl.when(target != e)
        def _():
            ret_remote(n, target).start()

        return 0

    lax.fori_loop(0, chips, send_ret, 0)

    small_wait(rs_buf, n_items - 1, small_recv.at[3])
    red = de_src[i]
    for k in range(n_items - 1):
        red = red + rs_buf[k]
    ar_src[...] = red
    to_events(ar_src, ar_buf, 4)

    pltpu.make_async_copy(mixbuf, mixbuf, ret_rsem).wait()
    scale = 1.0 / LENGTH
    tot = jnp.zeros((rows, 1), F32)
    for h in range(HEADS):
        tot = tot + jnp.sum(mixbuf[h].astype(F32), axis=1, keepdims=True)
    mean = tot * (1.0 / width)
    var = jnp.zeros((rows, 1), F32)
    for h in range(HEADS):
        c_h = (mixbuf[h].astype(F32) - mean) * scale
        var = var + jnp.sum(c_h * c_h, axis=1, keepdims=True)
    spread = lax.rsqrt(var * (1.0 / width) + EPS) * scale
    gated = jnp.concatenate(
        [
            ((mixbuf[h].astype(F32) - mean) * spread * ogain_ref[:, cols(h)] * gate_u[:, cols(h)]).astype(BF16)
            for h in range(HEADS)
        ],
        axis=1,
    )
    layer_ref[...] = (summed[...] + dot(gated, wo[...])).astype(BF16)

    out_layer = pltpu.make_async_copy(layer_ref, layer_out.at[0], out_sem.at[0])
    out_layer.start()

    small_wait(ar_buf, n_events - 1, small_recv.at[4])
    total = ar_src[...]
    for k in range(n_events - 1):
        total = total + ar_buf[k]
    dgated = to_compact(dot(to_rows(total).astype(BF16), wo[...], 1, 1))
    s_c = dgated * gate_c * ogain_c_ref[...]
    dmixed = (
        s_c - mean_all(s_c, width) - normal_c * mean_all(s_c * normal_c, width)
    ) * spread_c
    diag = jnp.concatenate([jnp.where(sub == h, dmixed, 0.0) for h in range(8)], axis=1)
    hi = diag.astype(BF16)
    lo = (diag - hi.astype(F32)).astype(BF16)
    w2 = jnp.concatenate([w_last.astype(F32), w_last.astype(F32)], axis=0).astype(BF16)
    hilo = jnp.concatenate([hi.astype(F32), lo.astype(F32)], axis=0).astype(BF16)
    dval_ref[...] = dot(w2, hilo, 0, 0)

    out_dval = pltpu.make_async_copy(dval_ref, dval_out.at[0], out_sem.at[2])
    out_dval.start()

    small_wait(last_buf, n_events - 1, small_send.at[0])
    small_wait(part_buf, n_events - 1, small_send.at[1])
    small_wait(user_buf, n_items - 1, small_send.at[2])
    small_wait(rs_buf, n_items - 1, small_send.at[3])
    small_wait(ar_buf, n_events - 1, small_send.at[4])
    kv_part = kv_send.at[pl.ds(0, chips - 1)]
    pltpu.make_async_copy(kv_part, kv_part, kv_ssem).wait()
    pltpu.make_async_copy(kv_send, kv_send, fwd_ssem).wait()
    q_part = q_send.at[pl.ds(0, chips - 1)]
    pltpu.make_async_copy(q_part, q_part, q_ssem).wait()

    @pl.when(owner != core)
    def _():
        q_remote(my_chip).wait_send()

    def ret_wait(n, _):
        target = ret_target(n)

        @pl.when(target != e)
        def _():
            ret_remote(n, target).wait_send()

        return 0

    lax.fori_loop(0, chips, ret_wait, 0)
    out_scores.wait()
    out_dval.wait()
    out_layer.wait()


def local(
    n_items,
    n_events,
    history,
    actions,
    action_table,
    lengths,
    input_gain,
    input_weight,
    output_gain,
    output_weight,
    item_codes,
    item_scale,
    gate_first,
    gate_second,
    teacher,
):
    _, rows, width = history.shape
    chips = n_events // 2
    items = item_codes.shape[0]
    users = n_items
    small = (8, LANES)
    smem = pl.BlockSpec(memory_space=pltpu.SMEM)
    hbm = pl.BlockSpec(memory_space=pl.ANY)
    dma = pltpu.SemaphoreType.DMA
    layer, scores, dvalues = pl.pallas_call(
        functools.partial(kernel, n_items, n_events),
        out_shape=(
            jax.ShapeDtypeStruct((1, rows, width), BF16),
            jax.ShapeDtypeStruct((users, items), F32),
            jax.ShapeDtypeStruct((1, rows, width), F32),
        ),
        in_specs=[smem] + [hbm] * 14,
        out_specs=(hbm, hbm, hbm),
        scratch_shapes=[
            pltpu.VMEM((rows, width), BF16),
            pltpu.VMEM(actions.shape, jnp.int32),
            pltpu.VMEM(action_table.shape, BF16),
            pltpu.VMEM((1, width), F32),
            pltpu.VMEM((8, LANES), F32),
            pltpu.VMEM((1, width), F32),
            pltpu.VMEM((8, LANES), F32),
            pltpu.VMEM((ITEM_COMPS, items), F32),
            pltpu.VMEM(gate_first.shape, BF16),
            pltpu.VMEM(gate_first.shape, BF16),
            pltpu.VMEM((users, items), F32),
            pltpu.VMEM(item_codes.shape, jnp.int32),
            pltpu.VMEM((width, width), BF16),
            pltpu.VMEM((4 * width // CHUNK, width, CHUNK), BF16),
            pltpu.VMEM((rows, width), BF16),
            pltpu.VMEM((users, items), F32),
            pltpu.VMEM((rows, width), F32),
            dma((3,)),
            dma((13,)),
            dma((4 * width // CHUNK,)),
            pltpu.VMEM((rows, width), F32),
            pltpu.VMEM((rows + 16, width), BF16),
            pltpu.VMEM((rows, width), F32),
            pltpu.VMEM((HEADS, 2, rows, LANES), BF16),
            pltpu.VMEM((HEADS, rows, LANES), BF16),
            pltpu.VMEM((n_events, 2, rows, LANES), BF16),
            pltpu.VMEM((chips, rows, LANES), BF16),
            pltpu.VMEM((chips, rows, LANES), BF16),
            pltpu.VMEM((HEADS, rows, LANES), BF16),
            pltpu.VMEM(small, F32),
            pltpu.VMEM((n_events - 1,) + small, F32),
            pltpu.VMEM(small, F32),
            pltpu.VMEM((n_events - 1,) + small, F32),
            pltpu.VMEM(small, F32),
            pltpu.VMEM((n_items,) + small, F32),
            pltpu.VMEM((n_items,) + small, F32),
            pltpu.VMEM((n_items - 1,) + small, F32),
            pltpu.VMEM(small, F32),
            pltpu.VMEM((n_events - 1,) + small, F32),
            pltpu.VMEM((COMPS * ITEM_COMPS, users * LANES), F32),
            pltpu.VMEM((users * 8, ITEM_COMPS * items), F32),
            pltpu.VMEM((LANES, ITEM_COMPS * items), BF16),
            pltpu.VMEM((ITEM_COMPS * items, LANES), BF16),
            dma((5,)),
            dma((5,)),
            dma(()),
            dma(()),
            dma((chips,)),
            dma(()),
            dma(()),
            dma(()),
            dma(()),
            dma(()),
            dma(()),
        ],
        compiler_params=pltpu.CompilerParams(
            collective_id=0, has_side_effects=True, vmem_limit_bytes=VMEM_LIMIT
        ),
    )(
        lengths,
        history,
        actions,
        action_table,
        input_gain.reshape(1, width),
        input_gain.reshape(8, LANES),
        output_gain.reshape(1, width),
        output_gain.reshape(8, LANES),
        item_scale.T,
        gate_first,
        gate_second.T,
        teacher,
        item_codes,
        output_weight,
        input_weight,
    )
    return pl.pallas_call(
        write_out,
        out_shape=(
            jax.ShapeDtypeStruct((1, rows, width), BF16),
            jax.ShapeDtypeStruct((users, items), F32),
            jax.ShapeDtypeStruct((1, rows, width), F32),
        ),
        in_specs=[pl.BlockSpec(memory_space=pl.ANY)] * 3,
        out_specs=(hbm, hbm, hbm),
        scratch_shapes=[
            pltpu.VMEM((1, rows, width), BF16),
            pltpu.VMEM((users, items), F32),
            pltpu.VMEM((1, rows, width), F32),
            dma((2, 3)),
        ],
        compiler_params=pltpu.CompilerParams(vmem_limit_bytes=VMEM_LIMIT),
    )(layer, scores, dvalues)


def write_out(layer_in, scores_in, dval_in, layer_out, scores_out, dval_out, layer, scores, dval, sem):
    trips = ((dval_in, dval, dval_out), (layer_in, layer, layer_out), (scores_in, scores, scores_out))
    reads = [pltpu.make_async_copy(a, b, sem.at[0, k]) for k, (a, b, _) in enumerate(trips)]
    writes = [pltpu.make_async_copy(b, c, sem.at[1, k]) for k, (_, b, c) in enumerate(trips)]
    for copy in reads:
        copy.start()
    for first, second in zip(reads, writes):
        first.wait()
        second.start()
    for copy in writes:
        copy.wait()


def solution(mesh):
    in_specs = (
        P("items", "events", None),
        P("items", "events"),
        P(),
        P("items"),
        P(),
        P(),
        P(),
        P(),
        P(("items", "events"), None),
        P(("items", "events"), None),
        P(),
        P(),
        P(None, ("items", "events")),
    )
    out_specs = (
        P("items", "events", None),
        P(None, ("items", "events")),
        P("items", "events", None),
    )
    body = functools.partial(local, mesh.shape["items"], mesh.shape["events"])
    return jax.shard_map(body, mesh=mesh, in_specs=in_specs, out_specs=out_specs, check_vma=False)
```

```python
import functools

import jax
import jax.numpy as jnp
from jax import lax
from jax.experimental import pallas as pl
from jax.experimental.pallas import tpu as pltpu
from jax.sharding import PartitionSpec as P

MESH = pl.DeviceIdType.MESH
HEADS = 8
COMPS = 8
ITEM_COMPS = 8
LENGTH = 2048
LANES = 128
EPS = 1e-05
F32, BF16 = jnp.float32, jnp.bfloat16
CHUNK = 512
GROUP = 16
VMEM_LIMIT = 64 * 1000 * 1000
ORDER = (4, 6, 5, 7, 2, 3, 0, 1)


def dot(a, b, ca=1, cb=0):
    return lax.dot_general(a, b, (((ca,), (cb,)), ((), ())), preferred_element_type=F32)


def silu(v):
    half = 0.5 * v
    return half * jnp.tanh(half) + half


def sigmoid(v):
    return 0.5 * jnp.tanh(0.5 * v) + 0.5


def iota(shape, dim):
    return lax.broadcasted_iota(jnp.int32, shape, dim)


def cols(h):
    return slice(h * LANES, (h + 1) * LANES)


def mean_all(v, count):
    return jnp.sum(jnp.sum(v, axis=1, keepdims=True), axis=0, keepdims=True) * (1.0 / count)


def to_rows(c):
    return jnp.concatenate([jnp.broadcast_to(c[h : h + 1, :], (8, LANES)) for h in range(8)], axis=1)


def to_compact(rows):
    sub = iota((8, LANES), 0)
    out = jnp.zeros((8, LANES), F32)
    for h in range(8):
        out = out + jnp.where(sub == h, rows[:, cols(h)], 0.0)
    return out


def kernel(
    n_items,
    n_events,
    lengths_ref,
    hist_in,
    actions_in,
    table_in,
    igain_in,
    igain_c_in,
    ogain_in,
    ogain_c_in,
    scale_in,
    g1_in,
    g2t_in,
    teacher_in,
    codes_in,
    wo_in,
    w_in,
    layer_out,
    scores_out,
    dval_out,
    hist,
    actions_ref,
    table,
    igain_ref,
    igain_c_ref,
    ogain_ref,
    ogain_c_ref,
    scale_ref,
    g1_ref,
    g2t_ref,
    teacher_ref,
    codes,
    wo,
    w,
    layer_ref,
    scores_ref,
    dval_ref,
    out_sem,
    in_sem,
    w_sem,
    summed,
    lhs,
    gate_u,
    kv_send,
    q_send,
    kv_all,
    q_all,
    mret,
    mixbuf,
    last_src,
    last_buf,
    part_src,
    part_buf,
    user_src,
    user_buf,
    de_src,
    rs_buf,
    ar_src,
    ar_buf,
    lref,
    dref,
    items_t,
    items_n,
    wo_t,
    small_send,
    small_recv,
    loc_sem,
    kv_ssem,
    kv_rsem,
    q_ssem,
    q_rsem,
    fwd_ssem,
    fwd_rsem,
    ret_ssem,
    ret_rsem,
):
    i = lax.axis_index("items")
    e = lax.axis_index("events")
    chips = n_events // 2
    my_chip, core = e // 2, e % 2
    sibling = 2 * my_chip + (1 - core)
    rows = hist.shape[0]
    width = hist.shape[1]
    length = lengths_ref[0]

    pairs = (
        (hist_in.at[0], hist),
        (actions_in, actions_ref),
        (table_in, table),
        (igain_in, igain_ref),
        (igain_c_in, igain_c_ref),
        (ogain_in, ogain_ref),
        (ogain_c_in, ogain_c_ref),
        (scale_in, scale_ref),
        (g1_in, g1_ref),
        (g2t_in, g2t_ref),
        (teacher_in, teacher_ref),
        (codes_in, codes),
        (wo_in, wo),
    )
    loads = [pltpu.make_async_copy(a, b, in_sem.at[k]) for k, (a, b) in enumerate(pairs)]
    wloads = {
        c: pltpu.make_async_copy(
            w_in.at[:, pl.ds(c * CHUNK, CHUNK)], w.at[c], w_sem.at[c]
        )
        for c in ORDER
    }
    for k in range(12):
        loads[k].start()
    for c in ORDER:
        wloads[c].start()
    loads[12].start()

    barrier = pltpu.get_barrier_semaphore()

    def greet_events(k, _):
        pl.semaphore_signal(
            barrier, inc=1, device_id=(i, lax.rem(e + k, n_events)), device_id_type=MESH
        )
        return 0

    def greet_items(k, _):
        pl.semaphore_signal(
            barrier, inc=1, device_id=(lax.rem(i + k, n_items), e), device_id_type=MESH
        )
        return 0

    lax.fori_loop(1, n_events, greet_events, 0)
    lax.fori_loop(1, n_items, greet_items, 0)

    def to_events(src, buf, phase):
        def go(k, _):
            pltpu.make_async_remote_copy(
                src_ref=src,
                dst_ref=buf.at[k - 1],
                send_sem=small_send.at[phase],
                recv_sem=small_recv.at[phase],
                device_id=(i, lax.rem(e + k, n_events)),
                device_id_type=MESH,
            ).start()
            return 0

        lax.fori_loop(1, n_events, go, 0)

    def small_wait(buf, count, sem):
        part = buf.at[pl.ds(0, count)]
        pltpu.make_async_copy(part, part, sem).wait()

    for k in range(5):
        loads[k].wait()
    onehot_t = (iota((16, rows), 0) == jnp.broadcast_to(actions_ref[...], (16, rows))).astype(BF16)
    s_val = hist[...].astype(F32) + dot(onehot_t, table[...], 0, 0)
    summed[...] = s_val
    at_last = (iota((rows, LANES), 0) + e * rows) == (length - 1)
    picked = jnp.concatenate(
        [jnp.sum(jnp.where(at_last, s_val[:, cols(h)], 0.0), axis=0, keepdims=True) for h in range(8)],
        axis=0,
    )
    last_src[...] = picked
    center = s_val - jnp.mean(s_val, axis=1, keepdims=True)
    spread = lax.rsqrt(jnp.mean(center * center, axis=1, keepdims=True) + EPS)
    lhs[pl.ds(0, rows), :] = (center * spread * igain_ref[...]).astype(BF16)

    pl.semaphore_wait(barrier, n_events - 1 + n_items - 1)
    to_events(last_src, last_buf, 0)

    for k in range(5, 12):
        loads[k].wait()
    p_i, q_i = iota((512, 512), 0), iota((512, 512), 1)
    expand = jnp.where(p_i == 4 * (q_i & 127) + (q_i >> 7), 1.0, 0.0).astype(BF16)
    for half in range(2):
        words = codes[:, cols(half)]
        nibbles = jnp.concatenate(
            [(((words >> (4 * n)) & 15).astype(F32) - 7.5).astype(BF16) for n in range(4)], axis=1
        )
        raw = dot(expand, nibbles, 1, 1)
        for j in range(4):
            c = half * 4 + j
            vector = raw[j * LANES : (j + 1) * LANES] * scale_ref[c : c + 1, :]
            items_t[:, cols(c)] = vector.astype(BF16)
            items_n[c * LANES : (c + 1) * LANES, :] = vector.T.astype(BF16)
    logit_count = COMPS * ITEM_COMPS
    r_i, s_i = iota((logit_count, logit_count), 0), iota((logit_count, logit_count), 1)
    perm = jnp.where(s_i == (r_i & 7) * 8 + (r_i >> 3), 1.0, 0.0).astype(BF16)
    g1, g2t = g1_ref[...], g2t_ref[...]
    m_first_t = dot(g1, perm, 0, 1).astype(BF16)
    m_first = dot(perm, g1).astype(BF16)
    m_second_t = dot(perm, g2t).astype(BF16)
    m_second = dot(g2t, perm, 0, 1).astype(BF16)

    normed = lhs[pl.ds(0, rows), :]
    keep_row = (iota((rows, LANES), 0) + e * rows) < length
    for c in (4, 6, 5, 7):
        wloads[c].wait()
        y = silu(dot(normed, w[c]))
        for j in range(CHUNK // LANES):
            head = (c % 2) * (CHUNK // LANES) + j
            block = y[:, cols(j)]
            if c < 6:
                kv_send[head, 0] = block.astype(BF16)
            else:
                kv_send[head, 1] = jnp.where(keep_row, block, 0.0).astype(BF16)

    owner = lax.rem(e + my_chip, 2)

    def kv_copy(k, target_core, block, sem_s, sem_r):
        chip = lax.rem(my_chip + k, chips)
        return pltpu.make_async_remote_copy(
            src_ref=kv_send.at[chip],
            dst_ref=kv_all.at[block],
            send_sem=sem_s,
            recv_sem=sem_r,
            device_id=(i, 2 * chip + target_core),
            device_id_type=MESH,
        )

    own_kv = pltpu.make_async_copy(kv_send.at[my_chip], kv_all.at[e], loc_sem)
    own_kv.start()
    sib_kv = pltpu.make_async_remote_copy(
        src_ref=kv_send.at[my_chip],
        dst_ref=kv_all.at[e],
        send_sem=fwd_ssem,
        recv_sem=fwd_rsem,
        device_id=(i, sibling),
        device_id_type=MESH,
    )
    sib_kv.start()

    def send_kv(k, _):
        kv_copy(k, core, e, kv_ssem, kv_rsem.at[k]).start()
        return 0

    lax.fori_loop(1, chips, send_kv, 0)


    small_wait(last_buf, n_events - 1, small_recv.at[0])
    summed_c = last_src[...]
    for k in range(n_events - 1):
        summed_c = summed_c + last_buf[k]
    center = summed_c - mean_all(summed_c, width)
    spread = lax.rsqrt(mean_all(center * center, width) + EPS)
    last_rows = to_rows(center * spread * igain_c_ref[...])
    lhs[pl.ds(rows, 16), :] = jnp.concatenate([last_rows, last_rows], axis=0).astype(BF16)

    both = lhs[...]
    sub = iota((8, LANES), 0)
    q_diag = []
    for c in (2, 3):
        wloads[c].wait()
        y = silu(dot(both, w[c]))
        for j in range(CHUNK // LANES):
            head = (c % 2) * (CHUNK // LANES) + j
            q_send[head] = y[:rows, cols(j)].astype(BF16)
            q_diag.append(jnp.where(sub == head, y[rows : rows + 8, cols(j)], 0.0))

    inv = width // HEADS
    all_keys = jnp.concatenate([kv_send[head, 0] for head in range(HEADS)], axis=1)
    all_values = jnp.concatenate([kv_send[head, 1] for head in range(HEADS)], axis=1)
    q_scores = dot(jnp.concatenate(q_diag, axis=1).astype(BF16), all_keys, 1, 1)
    keep_col = (iota((8, rows), 1) + e * rows) < length
    w_last = jnp.where(keep_col, silu(q_scores * inv ** (-0.5)) * (1.0 / LENGTH), 0.0).astype(BF16)
    part_src[...] = to_compact(dot(w_last, all_values))
    to_events(part_src, part_buf, 1)

    gate_rows = []
    for c in (0, 1):
        wloads[c].wait()
        y = silu(dot(both, w[c]))
        gate_u[:, c * CHUNK : (c + 1) * CHUNK] = y[:rows]
        gate_rows.append(y[rows : rows + 8])
    gate_c = to_compact(jnp.concatenate(gate_rows, axis=1))

    small_wait(part_buf, n_events - 1, small_recv.at[1])
    mixed_c = part_src[...]
    for k in range(n_events - 1):
        mixed_c = mixed_c + part_buf[k]
    center_c = mixed_c - mean_all(mixed_c, width)
    spread_c = lax.rsqrt(mean_all(center_c * center_c, width) + EPS)
    normal_c = center_c * spread_c
    gated_c = normal_c * ogain_c_ref[...] * gate_c
    loads[12].wait()
    user_rows = dot(to_rows(gated_c).astype(BF16), wo[...])
    user_c = (summed_c + to_compact(user_rows)).astype(BF16).astype(F32)
    user_src[...] = user_c
    user_buf[i] = user_c

    def send_user(k, _):
        pltpu.make_async_remote_copy(
            src_ref=user_src,
            dst_ref=user_buf.at[i],
            send_sem=small_send.at[2],
            recv_sem=small_recv.at[2],
            device_id=(lax.rem(i + k, n_items), e),
            device_id_type=MESH,
        ).start()
        return 0

    lax.fori_loop(1, n_items, send_user, 0)

    def q_remote(chip):
        return pltpu.make_async_remote_copy(
            src_ref=q_send.at[chip],
            dst_ref=q_all.at[my_chip],
            send_sem=q_ssem,
            recv_sem=q_rsem,
            device_id=(i, 2 * chip + owner),
            device_id_type=MESH,
        )

    def send_q(k, _):
        q_remote(lax.rem(my_chip + k, chips)).start()
        return 0

    lax.fori_loop(1, chips, send_q, 0)

    @pl.when(owner == core)
    def _():
        pltpu.make_async_copy(q_send.at[my_chip], q_all.at[my_chip], q_rsem).start()

    @pl.when(owner != core)
    def _():
        q_remote(my_chip).start()

    own_kv.wait()

    def forward(k, _):
        source = 2 * lax.rem(my_chip + chips - k, chips) + core
        pltpu.make_async_copy(kv_all.at[source], kv_all.at[source], kv_rsem.at[k]).wait()
        pltpu.make_async_remote_copy(
            src_ref=kv_all.at[source],
            dst_ref=kv_all.at[source],
            send_sem=fwd_ssem,
            recv_sem=fwd_rsem,
            device_id=(i, sibling),
            device_id_type=MESH,
        ).start()
        return 0

    lax.fori_loop(1, chips, forward, 0)


    wo_t[...] = wo[...].T
    users = n_items
    small_wait(user_buf, n_items - 1, small_recv.at[2])
    everyone = user_buf[...].reshape(users * 8, LANES).astype(BF16)
    part_l = dot(everyone, items_t[...])
    for c in range(ITEM_COMPS):
        for b in range(users):
            lref[c * 8 : (c + 1) * 8, cols(b)] = part_l[b * 8 : (b + 1) * 8, cols(c)]
    for b0 in range(0, users, GROUP):
        logits = lref[:, b0 * LANES : (b0 + GROUP) * LANES]
        pre = dot(m_first_t, logits.astype(BF16))
        sig = sigmoid(pre)
        gates = sigmoid(dot(m_second_t, (pre * sig).astype(BF16)))
        gl = gates * logits
        score = jnp.sum(gl, axis=0, keepdims=True)
        targets = jnp.concatenate([teacher_ref[b0 + j : b0 + j + 1, :] for j in range(GROUP)], axis=1)
        slope = (gl * (1.0 - gates)).astype(BF16)
        back = dot(m_second, slope) * (sig * (1.0 + pre * (1.0 - sig)))
        dlog = (score - targets) * (gates + dot(m_first, back.astype(BF16)))
        for j in range(GROUP):
            b = b0 + j
            scores_ref[b : b + 1, :] = score[:, cols(j)]
            for c in range(ITEM_COMPS):
                dref[b * 8 : (b + 1) * 8, cols(c)] = dlog[c * 8 : (c + 1) * 8, cols(j)]
    demb = dot(dref[...].astype(BF16), items_n[...])
    de_src[...] = demb.reshape(users, 8, LANES)

    def send_de(k, _):
        other = lax.rem(i + k, n_items)
        pltpu.make_async_remote_copy(
            src_ref=de_src.at[other],
            dst_ref=rs_buf.at[k - 1],
            send_sem=small_send.at[3],
            recv_sem=small_recv.at[3],
            device_id=(other, e),
            device_id_type=MESH,
        ).start()
        return 0

    lax.fori_loop(1, n_items, send_de, 0)

    out_scores = pltpu.make_async_copy(scores_ref, scores_out, out_sem.at[1])
    out_scores.start()

    half_blocks = kv_all.at[pl.ds(0, chips)]
    pltpu.make_async_copy(half_blocks, half_blocks, fwd_rsem).wait()
    pltpu.make_async_copy(q_all, q_all, q_rsem).wait()
    half_scale = 0.5 * inv ** (-0.5)
    for n in range(chips):
        query = q_all[n]
        odd = lax.rem(core + n, 2)
        acc = jnp.zeros((rows, LANES), F32)
        for m in range(n + 1):
            key = jnp.concatenate([kv_all[2 * m, 0], kv_all[2 * m + 1, 0]], axis=0)
            value = jnp.concatenate([kv_all[2 * m, 1], kv_all[2 * m + 1, 1]], axis=0)
            half = dot(query, key, 1, 1) * half_scale
            weight = half * jnp.tanh(half) + half
            if m == n:
                causal = iota((rows, 2 * rows), 1) <= iota((rows, 2 * rows), 0) + odd * rows
                weight = jnp.where(causal, weight, 0.0)
            acc = acc + dot(weight.astype(BF16), value)
        mret[n] = acc.astype(BF16)

    def ret_remote(n, target):
        return pltpu.make_async_remote_copy(
            src_ref=mret.at[n],
            dst_ref=mixbuf.at[my_chip],
            send_sem=ret_ssem,
            recv_sem=ret_rsem,
            device_id=(i, target),
            device_id_type=MESH,
        )

    def ret_target(n):
        return 2 * n + lax.rem(n + core, 2)

    def send_ret(n, _):
        target = ret_target(n)

        @pl.when(target == e)
        def _():
            pltpu.make_async_copy(mret.at[n], mixbuf.at[my_chip], ret_rsem).start()

        @pl.when(target != e)
        def _():
            ret_remote(n, target).start()

        return 0

    lax.fori_loop(0, chips, send_ret, 0)

    small_wait(rs_buf, n_items - 1, small_recv.at[3])
    red = de_src[i]
    for k in range(n_items - 1):
        red = red + rs_buf[k]
    ar_src[...] = red
    to_events(ar_src, ar_buf, 4)

    pltpu.make_async_copy(mixbuf, mixbuf, ret_rsem).wait()
    scale = 1.0 / LENGTH
    tot = jnp.zeros((rows, 1), F32)
    for h in range(HEADS):
        tot = tot + jnp.sum(mixbuf[h].astype(F32), axis=1, keepdims=True)
    mean = tot * (1.0 / width)
    var = jnp.zeros((rows, 1), F32)
    for h in range(HEADS):
        c_h = (mixbuf[h].astype(F32) - mean) * scale
        var = var + jnp.sum(c_h * c_h, axis=1, keepdims=True)
    spread = lax.rsqrt(var * (1.0 / width) + EPS) * scale
    gated = jnp.concatenate(
        [
            ((mixbuf[h].astype(F32) - mean) * spread * ogain_ref[:, cols(h)] * gate_u[:, cols(h)]).astype(BF16)
            for h in range(HEADS)
        ],
        axis=1,
    )
    layer_ref[...] = (summed[...] + dot(gated, wo[...])).astype(BF16)

    out_layer = pltpu.make_async_copy(layer_ref, layer_out.at[0], out_sem.at[0])
    out_layer.start()

    small_wait(ar_buf, n_events - 1, small_recv.at[4])
    total = ar_src[...]
    for k in range(n_events - 1):
        total = total + ar_buf[k]
    dgated = to_compact(dot(to_rows(total).astype(BF16), wo_t[...]))
    s_c = dgated * gate_c * ogain_c_ref[...]
    dmixed = (
        s_c - mean_all(s_c, width) - normal_c * mean_all(s_c * normal_c, width)
    ) * spread_c
    diag = jnp.concatenate([jnp.where(sub == h, dmixed, 0.0) for h in range(8)], axis=1)
    hi = diag.astype(BF16)
    lo = (diag - hi.astype(F32)).astype(BF16)
    w2 = jnp.concatenate([w_last.astype(F32), w_last.astype(F32)], axis=0).astype(BF16)
    hilo = jnp.concatenate([hi.astype(F32), lo.astype(F32)], axis=0).astype(BF16)
    dval_ref[...] = dot(w2, hilo, 0, 0)

    out_dval = pltpu.make_async_copy(dval_ref, dval_out.at[0], out_sem.at[2])
    out_dval.start()

    small_wait(last_buf, n_events - 1, small_send.at[0])
    small_wait(part_buf, n_events - 1, small_send.at[1])
    small_wait(user_buf, n_items - 1, small_send.at[2])
    small_wait(rs_buf, n_items - 1, small_send.at[3])
    small_wait(ar_buf, n_events - 1, small_send.at[4])
    kv_part = kv_send.at[pl.ds(0, chips - 1)]
    pltpu.make_async_copy(kv_part, kv_part, kv_ssem).wait()
    pltpu.make_async_copy(kv_send, kv_send, fwd_ssem).wait()
    q_part = q_send.at[pl.ds(0, chips - 1)]
    pltpu.make_async_copy(q_part, q_part, q_ssem).wait()

    @pl.when(owner != core)
    def _():
        q_remote(my_chip).wait_send()

    def ret_wait(n, _):
        target = ret_target(n)

        @pl.when(target != e)
        def _():
            ret_remote(n, target).wait_send()

        return 0

    lax.fori_loop(0, chips, ret_wait, 0)
    out_scores.wait()
    out_dval.wait()
    out_layer.wait()


def local(
    n_items,
    n_events,
    history,
    actions,
    action_table,
    lengths,
    input_gain,
    input_weight,
    output_gain,
    output_weight,
    item_codes,
    item_scale,
    gate_first,
    gate_second,
    teacher,
):
    _, rows, width = history.shape
    chips = n_events // 2
    items = item_codes.shape[0]
    users = n_items
    small = (8, LANES)
    smem = pl.BlockSpec(memory_space=pltpu.SMEM)
    hbm = pl.BlockSpec(memory_space=pl.ANY)
    dma = pltpu.SemaphoreType.DMA
    layer, scores, dvalues = pl.pallas_call(
        functools.partial(kernel, n_items, n_events),
        out_shape=(
            jax.ShapeDtypeStruct((1, rows, width), BF16),
            jax.ShapeDtypeStruct((users, items), F32),
            jax.ShapeDtypeStruct((1, rows, width), F32),
        ),
        in_specs=[smem] + [hbm] * 14,
        out_specs=(hbm, hbm, hbm),
        scratch_shapes=[
            pltpu.VMEM((rows, width), BF16),
            pltpu.VMEM(actions.shape, jnp.int32),
            pltpu.VMEM(action_table.shape, BF16),
            pltpu.VMEM((1, width), F32),
            pltpu.VMEM((8, LANES), F32),
            pltpu.VMEM((1, width), F32),
            pltpu.VMEM((8, LANES), F32),
            pltpu.VMEM((ITEM_COMPS, items), F32),
            pltpu.VMEM(gate_first.shape, BF16),
            pltpu.VMEM(gate_first.shape, BF16),
            pltpu.VMEM((users, items), F32),
            pltpu.VMEM(item_codes.shape, jnp.int32),
            pltpu.VMEM((width, width), BF16),
            pltpu.VMEM((4 * width // CHUNK, width, CHUNK), BF16),
            pltpu.VMEM((rows, width), BF16),
            pltpu.VMEM((users, items), F32),
            pltpu.VMEM((rows, width), F32),
            dma((3,)),
            dma((13,)),
            dma((4 * width // CHUNK,)),
            pltpu.VMEM((rows, width), F32),
            pltpu.VMEM((rows + 16, width), BF16),
            pltpu.VMEM((rows, width), F32),
            pltpu.VMEM((HEADS, 2, rows, LANES), BF16),
            pltpu.VMEM((HEADS, rows, LANES), BF16),
            pltpu.VMEM((n_events, 2, rows, LANES), BF16),
            pltpu.VMEM((chips, rows, LANES), BF16),
            pltpu.VMEM((chips, rows, LANES), BF16),
            pltpu.VMEM((HEADS, rows, LANES), BF16),
            pltpu.VMEM(small, F32),
            pltpu.VMEM((n_events - 1,) + small, F32),
            pltpu.VMEM(small, F32),
            pltpu.VMEM((n_events - 1,) + small, F32),
            pltpu.VMEM(small, F32),
            pltpu.VMEM((n_items,) + small, F32),
            pltpu.VMEM((n_items,) + small, F32),
            pltpu.VMEM((n_items - 1,) + small, F32),
            pltpu.VMEM(small, F32),
            pltpu.VMEM((n_events - 1,) + small, F32),
            pltpu.VMEM((COMPS * ITEM_COMPS, users * LANES), F32),
            pltpu.VMEM((users * 8, ITEM_COMPS * items), F32),
            pltpu.VMEM((LANES, ITEM_COMPS * items), BF16),
            pltpu.VMEM((ITEM_COMPS * items, LANES), BF16),
            pltpu.VMEM((width, width), BF16),
            dma((5,)),
            dma((5,)),
            dma(()),
            dma(()),
            dma((chips,)),
            dma(()),
            dma(()),
            dma(()),
            dma(()),
            dma(()),
            dma(()),
        ],
        compiler_params=pltpu.CompilerParams(
            collective_id=0, has_side_effects=True, vmem_limit_bytes=VMEM_LIMIT
        ),
    )(
        lengths,
        history,
        actions,
        action_table,
        input_gain.reshape(1, width),
        input_gain.reshape(8, LANES),
        output_gain.reshape(1, width),
        output_gain.reshape(8, LANES),
        item_scale.T,
        gate_first,
        gate_second.T,
        teacher,
        item_codes,
        output_weight,
        input_weight,
    )
    return pl.pallas_call(
        write_out,
        out_shape=(
            jax.ShapeDtypeStruct((1, rows, width), BF16),
            jax.ShapeDtypeStruct((users, items), F32),
            jax.ShapeDtypeStruct((1, rows, width), F32),
        ),
        in_specs=[pl.BlockSpec(memory_space=pl.ANY)] * 3,
        out_specs=(hbm, hbm, hbm),
        scratch_shapes=[
            pltpu.VMEM((1, rows, width), BF16),
            pltpu.VMEM((users, items), F32),
            pltpu.VMEM((1, rows, width), F32),
            dma((2, 3)),
        ],
        compiler_params=pltpu.CompilerParams(vmem_limit_bytes=VMEM_LIMIT),
    )(layer, scores, dvalues)


def write_out(layer_in, scores_in, dval_in, layer_out, scores_out, dval_out, layer, scores, dval, sem):
    trips = ((dval_in, dval, dval_out), (layer_in, layer, layer_out), (scores_in, scores, scores_out))
    reads = [pltpu.make_async_copy(a, b, sem.at[0, k]) for k, (a, b, _) in enumerate(trips)]
    writes = [pltpu.make_async_copy(b, c, sem.at[1, k]) for k, (_, b, c) in enumerate(trips)]
    for copy in reads:
        copy.start()
    for first, second in zip(reads, writes):
        first.wait()
        second.start()
    for copy in writes:
        copy.wait()


def solution(mesh):
    in_specs = (
        P("items", "events", None),
        P("items", "events"),
        P(),
        P("items"),
        P(),
        P(),
        P(),
        P(),
        P(("items", "events"), None),
        P(("items", "events"), None),
        P(),
        P(),
        P(None, ("items", "events")),
    )
    out_specs = (
        P("items", "events", None),
        P(None, ("items", "events")),
        P("items", "events", None),
    )
    body = functools.partial(local, mesh.shape["items"], mesh.shape["events"])
    return jax.shard_map(body, mesh=mesh, in_specs=in_specs, out_specs=out_specs, check_vma=False)
```
